512 devices in a mesh: patch: 128 (over z, y, core), mp: 4 (over x).
Axes of the slice: x: 4, y: 8, z: 8, core: 2. Of those that a mesh axis runs over, the one named last changes fastest.
Arguments:
- points: bfloat16 [65536, 256], P(('patch', 'mp')), may hold values from -6 to 6
- patch_counts: int32 [128], replicated, may hold values from 256 to 512, as said below
- to_hilbert: int32 [65536], P('patch'), may hold values from 0 to 65535, as said below
- from_hilbert: int32 [65536], P('patch'), may hold values from 0 to 65535, as said below
- cotangent: bfloat16 [65536, 256], P(('patch', 'mp')), may hold values from -0.0625 to 0.0625
- gain_mixer: float32 [2, 256], replicated, may hold values from 0.5 to 1.5
- query_weight: bfloat16 [2, 256, 256], replicated, may hold values from -0.375 to 0.375
- key_weight: bfloat16 [2, 256, 256], replicated, may hold values from -0.375 to 0.375
- value_weight: bfloat16 [2, 256, 256], replicated, may hold values from -0.375 to 0.375
- out_weight: bfloat16 [2, 256, 256], replicated, may hold values from -0.375 to 0.375
- gain_feed: float32 [2, 256], replicated, may hold values from 0.5 to 1.5
- up_weight: bfloat16 [2, 256, 1024], replicated, may hold values from -0.375 to 0.375
- down_weight: bfloat16 [2, 1024, 256], replicated, may hold values from -0.1875 to 0.1875
Outputs:
- hilbert_out: bfloat16 [65536, 256], P(('patch', 'mp'))
- grad_gain_mixer: float32 [2, 256], replicated
- grad_query: float32 [2, 256, 256], P(None, 'mp')
- grad_key: float32 [2, 256, 256], P(None, 'mp')
- grad_value: float32 [2, 256, 256], P(None, 'mp')
- grad_out: float32 [2, 256, 256], P(None, 'mp')
- grad_gain_feed: float32 [2, 256], replicated
- grad_up: float32 [2, 256, 1024], P(None, 'mp')
- grad_down: float32 [2, 1024, 256], P(None, 'mp')
The draws below stay inside these ranges and needn't reach their ends.
Inputs may be any that keep to these rules, and one draw needn't show every extreme that they name: z-ordered patch i holds points in its first patch_counts[i] rows and padding in the rest. A permutation of the rows: z-ordered row r becomes Hilbert row to_hilbert[r]; of the 512 rows of one aligned block, at most 6 land in any one aligned block of 512 rows, and some pair of blocks reaches 6. `from_hilbert`: the inverse permutation of to_hilbert.
All inputs are finite; a program needn't handle non-finite values.
Results may differ from the reference program's by a relative error of at most 0.034.
Values may be sent and summed in bfloat16 or wider, within the bound.
No kernel may reach another device: no remote copies, remote signals or barrier semaphores. Data moves between devices by JAX's collectives and lax.ppermute only.
A program may use at most 64 MiB of HBM per device.

```python
import jax
import jax.numpy as jnp
from jax import lax

C = 256
HEADS = 16
HIDDEN_SIZE = 1024
PATCH = 512
BLOCKS = 2
PTS_DEV = 512
HEAD_DIM = 16
TOKENS = 65536
ZPATCHES = 128
N_PATCH = 128


def shared_pairing(key):
    peer_count = N_PATCH
    local_rows = PTS_DEV
    per_peer = local_rows // peer_count
    key_pair, key_spread, key_pick, key_label, key_rows = jax.random.split(key, 5)
    pairing = jax.random.permutation(key_pair, peer_count)
    spread = jax.random.randint(key_spread, (peer_count // 2,), 0, per_peer // 2 + 1)
    chosen = jax.random.randint(key_pick, (), 0, peer_count // 2)
    spread = jnp.where(jnp.arange(peer_count // 2) == chosen, per_peer // 2, spread)
    multiple = jnp.zeros((peer_count,), jnp.int32)
    multiple = multiple.at[pairing[0::2]].set(per_peer + spread)
    multiple = multiple.at[pairing[1::2]].set(per_peer - spread)
    offsets = jnp.repeat(jnp.arange(peer_count, dtype=jnp.int32), multiple, total_repeat_length=local_rows)
    labels = jax.random.permutation(key_label, peer_count)
    row_keys = jax.random.split(key_rows, 2 * peer_count)
    shuffles = jax.vmap(lambda one_key: jax.random.permutation(one_key, local_rows))(row_keys)
    source_shuffle = shuffles[:peer_count]
    target_shuffle = shuffles[peer_count:]
    entries = jnp.broadcast_to(jnp.arange(local_rows)[None, :], (peer_count, local_rows))
    target_label = jnp.arange(peer_count, dtype=jnp.int32)[:, None]
    source_dev = (target_label - offsets[None, :]) % peer_count
    target_dev = jnp.broadcast_to(labels[:, None], (peer_count, local_rows))
    source_row = source_shuffle[source_dev, entries]
    target_row = target_shuffle[target_dev, entries]
    source_global = (source_dev * local_rows + source_row).reshape(-1).astype(jnp.int32)
    target_global = (target_dev * local_rows + target_row).reshape(-1).astype(jnp.int32)
    return (source_global, target_global)


def draw_to_hilbert(key, part):
    source_global, target_global = shared_pairing(key)
    return jnp.zeros((TOKENS,), jnp.int32).at[source_global].set(target_global)


def draw_from_hilbert(key, part):
    source_global, target_global = shared_pairing(key)
    return jnp.zeros((TOKENS,), jnp.int32).at[target_global].set(source_global)


def draw_patch_counts(key, part):
    key = jax.random.fold_in(key, 5)
    key_base, key_top, key_low = jax.random.split(key, 3)
    counts = PATCH - jax.random.randint(key_base, (ZPATCHES,), 0, PATCH // 2 + 1)
    top_index = jax.random.randint(key_top, (), 0, ZPATCHES)
    low_index = (top_index + 1 + jax.random.randint(key_low, (), 0, ZPATCHES - 1)) % ZPATCHES
    counts = counts.at[top_index].set(PATCH).at[low_index].set(PATCH // 2)
    return counts.astype(jnp.int32)


def steps_of(rng, extent, pieces, low, largest):
    def one(position, parts):
        heights = jax.random.uniform(jax.random.fold_in(jax.random.fold_in(rng, 6), position), (parts,), jnp.float32, low / len(pieces), largest / len(pieces))
        return jnp.repeat(jnp.exp(heights), extent[position] // parts).reshape((-1,) + (1,) * (len(extent) - position - 1))

    loudness = one(*pieces[0])
    for cut in pieces[1:]:
        loudness = loudness * one(*cut)
    return loudness


def centred(key, extent, width, most, cuts=(), held_as=jnp.bfloat16):
    values = jax.random.normal(key, extent, jnp.float32) * width
    if len(cuts) > 0:
        values = steps_of(key, extent, cuts, -0.22, 0.18) * values
    return jnp.clip(values, min=-most, max=most).astype(held_as)


def setup_inputs(seed: int = 0) -> dict:
    key_list = jax.random.split(jax.random.key(seed), 14)
    points = centred(key_list[0], (TOKENS, C), 1.0, 6.0, ((0, 512),))
    patch_counts = draw_patch_counts(jax.random.fold_in(key_list[13], 71), 0)
    to_hilbert = draw_to_hilbert(jax.random.fold_in(key_list[13], 71), 0)
    from_hilbert = draw_from_hilbert(jax.random.fold_in(key_list[13], 71), 0)
    cotangent = centred(key_list[4], (TOKENS, C), (TOKENS ** -0.5), 0.0625, ((0, 512),))
    gain_mixer = jnp.clip(1.0 + 0.1 * jax.random.normal(key_list[5], (BLOCKS, C), jnp.float32), 0.5, 1.5)
    query_weight = centred(key_list[6], (BLOCKS, C, C), C ** -0.5, 0.375)
    key_weight = centred(key_list[7], (BLOCKS, C, C), C ** -0.5, 0.375)
    value_weight = centred(key_list[8], (BLOCKS, C, C), C ** -0.5, 0.375)
    out_weight = centred(key_list[9], (BLOCKS, C, C), C ** -0.5, 0.375)
    gain_feed = jnp.clip(1.0 + 0.1 * jax.random.normal(key_list[10], (BLOCKS, C), jnp.float32), 0.5, 1.5)
    up_weight = centred(key_list[11], (BLOCKS, C, HIDDEN_SIZE), C ** -0.5, 0.375)
    down_weight = centred(key_list[12], (BLOCKS, HIDDEN_SIZE, C), HIDDEN_SIZE ** -0.5, 0.1875)
    return {"points": points, "patch_counts": patch_counts, "to_hilbert": to_hilbert, "from_hilbert": from_hilbert, "cotangent": cotangent, "gain_mixer": gain_mixer, "query_weight": query_weight, "key_weight": key_weight, "value_weight": value_weight, "out_weight": out_weight, "gain_feed": gain_feed, "up_weight": up_weight, "down_weight": down_weight}


EPSILON = 1e-05
GELU_SCALE = 0.7978845608028654
GELU_CUBIC = 0.044715

def widen(values):
    return lax.optimization_barrier(values).astype(jnp.float32)

def norm_rows(values, gain_row):
    widened = values.astype(jnp.float32)
    centered = widened - lax.optimization_barrier(jnp.mean(widened, axis=1, keepdims=True))
    inverse = lax.rsqrt(lax.optimization_barrier(jnp.mean(centered * centered, axis=1, keepdims=True)) + EPSILON)
    normed = centered * inverse
    return (normed, inverse, (normed * gain_row[None, :]).astype(jnp.bfloat16))

def norm_back(grad_scaled, normed, inverse, gain_row):
    grad_gain = lax.optimization_barrier(jnp.sum(grad_scaled * normed, axis=0))
    grad_normed = grad_scaled * gain_row[None, :]
    centered = grad_normed - lax.optimization_barrier(jnp.mean(grad_normed, axis=1, keepdims=True))
    return (grad_gain, inverse * (centered - normed * lax.optimization_barrier(jnp.mean(grad_normed * normed, axis=1, keepdims=True))))

def gelu_pair(pre_act):
    cubed_part = pre_act * pre_act * pre_act
    tangent = jnp.tanh(GELU_SCALE * (pre_act + GELU_CUBIC * cubed_part))
    activated = 0.5 * pre_act * (1.0 + tangent)
    slopes = 0.5 * (1.0 + tangent) + 0.5 * pre_act * (1.0 - tangent * tangent) * GELU_SCALE * (1.0 + 3.0 * GELU_CUBIC * pre_act * pre_act)
    return (activated, slopes)

def allowed_keys(live_rows):
    patches = live_rows.shape[0] // PATCH
    live_grid = live_rows.reshape(patches, 1, PATCH) > 0
    diagonal = lax.broadcasted_iota(jnp.int32, (PATCH, PATCH), 0) == lax.broadcasted_iota(jnp.int32, (PATCH, PATCH), 1)
    return live_grid | diagonal[None, :, :]

def heads_first(matrix):
    return widen(matrix).reshape(PATCH, HEADS, HEAD_DIM).transpose(1, 0, 2)

def heads_last(stacked):
    return stacked.transpose(1, 0, 2).reshape(PATCH, HEADS * HEAD_DIM)

def patch_probability(query_head, key_head, allowed):
    scores = jnp.einsum('npd,nkd->npk', query_head, key_head) * HEAD_DIM ** (-0.5)
    weights = jnp.where(allowed, jnp.exp(scores), 0.0)
    return weights / lax.optimization_barrier(jnp.sum(weights, axis=2, keepdims=True))

def patch_forward(operands):
    query_p, key_p, value_p, live_p = operands
    allowed = allowed_keys(live_p)
    query_head, key_head, value_head = (heads_first(query_p), heads_first(key_p), heads_first(value_p))
    probability = patch_probability(query_head, key_head, allowed)
    lowered = widen(probability.astype(jnp.bfloat16))
    return heads_last(jnp.einsum('npk,nkd->npd', lowered, value_head).astype(jnp.bfloat16))

def patch_backward(operands):
    query_p, key_p, value_p, grad_p, live_p = operands
    allowed = allowed_keys(live_p)
    query_head, key_head, value_head = (heads_first(query_p), heads_first(key_p), heads_first(value_p))
    grad_head = heads_first(grad_p)
    probability = patch_probability(query_head, key_head, allowed)
    lowered = widen(probability.astype(jnp.bfloat16))
    grad_prob = jnp.einsum('npd,nkd->npk', grad_head, value_head)
    grad_value = jnp.einsum('npk,npd->nkd', lowered, grad_head).astype(jnp.bfloat16)
    inner_sum = lax.optimization_barrier(jnp.sum(probability * grad_prob, axis=2, keepdims=True))
    grad_score = widen((probability * (grad_prob - inner_sum) * HEAD_DIM ** (-0.5)).astype(jnp.bfloat16))
    grad_query = jnp.einsum('npk,nkd->npd', grad_score, key_head).astype(jnp.bfloat16)
    grad_key = jnp.einsum('npk,npd->nkd', grad_score, query_head).astype(jnp.bfloat16)
    return (heads_last(grad_query), heads_last(grad_key), heads_last(grad_value))

def by_patch(matrix):
    return matrix.reshape(ZPATCHES, PATCH, matrix.shape[1])

def block_forward(rows_in, live_rows, params):
    gain_mixer, query_weight, key_weight, value_weight, out_weight, gain_feed, up_weight, down_weight = params
    normed_a, inverse_a, scaled_a = norm_rows(rows_in, gain_mixer)
    query_m = jnp.dot(scaled_a, query_weight, preferred_element_type=jnp.float32).astype(jnp.bfloat16)
    key_m = jnp.dot(scaled_a, key_weight, preferred_element_type=jnp.float32).astype(jnp.bfloat16)
    value_m = jnp.dot(scaled_a, value_weight, preferred_element_type=jnp.float32).astype(jnp.bfloat16)
    heads_out = lax.map(patch_forward, (by_patch(query_m), by_patch(key_m), by_patch(value_m), live_rows.reshape(ZPATCHES, PATCH))).reshape(TOKENS, C)
    middle = (rows_in.astype(jnp.float32) + jnp.dot(heads_out, out_weight, preferred_element_type=jnp.float32)).astype(jnp.bfloat16)
    normed_m, inverse_m, scaled_m = norm_rows(middle, gain_feed)
    activated, slopes = gelu_pair(jnp.dot(scaled_m, up_weight, preferred_element_type=jnp.float32))
    hidden = activated.astype(jnp.bfloat16)
    block_out = (middle.astype(jnp.float32) + jnp.dot(hidden, down_weight, preferred_element_type=jnp.float32)).astype(jnp.bfloat16)
    kept_state = (normed_a, inverse_a, scaled_a, query_m, key_m, value_m, heads_out, normed_m, inverse_m, scaled_m, slopes, hidden, live_rows)
    return (block_out, kept_state)

def block_backward(grad_rows, kept_state, params):
    gain_mixer, query_weight, key_weight, value_weight, out_weight, gain_feed, up_weight, down_weight = params
    normed_a, inverse_a, scaled_a, query_m, key_m, value_m, heads_out, normed_m, inverse_m, scaled_m, slopes, hidden, live_rows = kept_state
    down_grad = jnp.dot(hidden.T, grad_rows, preferred_element_type=jnp.float32)
    grad_pre = (jnp.dot(grad_rows, down_weight.T, preferred_element_type=jnp.float32) * slopes).astype(jnp.bfloat16)
    up_grad = jnp.dot(scaled_m.T, grad_pre, preferred_element_type=jnp.float32)
    grad_scaled_m = jnp.dot(grad_pre, up_weight.T, preferred_element_type=jnp.float32)
    feed_gain_grad, grad_middle_norm = norm_back(grad_scaled_m, normed_m, inverse_m, gain_feed)
    grad_middle = (grad_rows.astype(jnp.float32) + grad_middle_norm).astype(jnp.bfloat16)
    out_grad = jnp.dot(heads_out.T, grad_middle, preferred_element_type=jnp.float32)
    grad_heads = jnp.dot(grad_middle, out_weight.T, preferred_element_type=jnp.float32).astype(jnp.bfloat16)
    grad_query, grad_key, grad_value = lax.map(patch_backward, (by_patch(query_m), by_patch(key_m), by_patch(value_m), by_patch(grad_heads), live_rows.reshape(ZPATCHES, PATCH)))
    grad_query = grad_query.reshape(TOKENS, C)
    grad_key = grad_key.reshape(TOKENS, C)
    grad_value = grad_value.reshape(TOKENS, C)
    query_grad = jnp.dot(scaled_a.T, grad_query, preferred_element_type=jnp.float32)
    key_grad = jnp.dot(scaled_a.T, grad_key, preferred_element_type=jnp.float32)
    value_grad = jnp.dot(scaled_a.T, grad_value, preferred_element_type=jnp.float32)
    grad_scaled_a = jnp.dot(grad_query, query_weight.T, preferred_element_type=jnp.float32) + jnp.dot(grad_key, key_weight.T, preferred_element_type=jnp.float32) + jnp.dot(grad_value, value_weight.T, preferred_element_type=jnp.float32)
    mixer_gain_grad, grad_in_norm = norm_back(grad_scaled_a, normed_a, inverse_a, gain_mixer)
    grad_in = (grad_middle.astype(jnp.float32) + grad_in_norm).astype(jnp.bfloat16)
    return ((mixer_gain_grad, query_grad, key_grad, value_grad, out_grad, feed_gain_grad, up_grad, down_grad), grad_in)

def reference(points, patch_counts, to_hilbert, from_hilbert, cotangent, gain_mixer, query_weight, key_weight, value_weight, out_weight, gain_feed, up_weight, down_weight):
    row_index = jnp.arange(TOKENS, dtype=jnp.int32)
    live_zorder = (row_index % PATCH < patch_counts[row_index // PATCH]).astype(jnp.int32)
    live_hilbert = live_zorder[from_hilbert]
    stacks = (gain_mixer, query_weight, key_weight, value_weight, out_weight, gain_feed, up_weight, down_weight)
    first_params = tuple((stacked[0] for stacked in stacks))
    second_params = tuple((stacked[1] for stacked in stacks))
    first_out, first_state = block_forward(points, live_zorder, first_params)
    second_in = first_out[from_hilbert]
    hilbert_out, second_state = block_forward(second_in, live_hilbert, second_params)
    second_grads, grad_second_in = block_backward(cotangent, second_state, second_params)
    grad_first_out = grad_second_in[to_hilbert]
    first_grads, unused_grad = block_backward(grad_first_out, first_state, first_params)
    joined = [jnp.stack([first_grads[member], second_grads[member]]) for member in range(8)]
    return (hilbert_out, joined[0], joined[1], joined[2], joined[3], joined[4], joined[5], joined[6], joined[7])
```

```python
import functools

import jax
import jax.numpy as jnp
from jax import lax
from jax.experimental import pallas as pl
from jax.experimental.pallas import tpu as pltpu
from jax.sharding import PartitionSpec as P

HEADS = 16
PATCH = 512
HEAD_DIM = 16
WIDTH = 256
HIDDEN = 1024
SLOTS = 8

EPSILON = 1e-05
GELU_SCALE = 0.7978845608028654
GELU_CUBIC = 0.044715

BF = jnp.bfloat16
F32 = jnp.float32


def dot(left, right, left_dim=1, right_dim=0):
    return lax.dot_general(
        left, right, (((left_dim,), (right_dim,)), ((), ())), preferred_element_type=F32
    )


def norm_rows(values, gain_row):
    widened = values.astype(F32)
    centered = widened - jnp.mean(widened, axis=1, keepdims=True)
    inverse = lax.rsqrt(jnp.mean(centered * centered, axis=1, keepdims=True) + EPSILON)
    normed = centered * inverse
    return normed, inverse, (normed * gain_row).astype(BF)


def norm_back(grad_scaled, normed, inverse, gain_row):
    grad_normed = grad_scaled * gain_row
    centered = grad_normed - jnp.mean(grad_normed, axis=1, keepdims=True)
    return inverse * (centered - normed * jnp.mean(grad_normed * normed, axis=1, keepdims=True))


def gelu(pre):
    tangent = jnp.tanh(GELU_SCALE * (pre + GELU_CUBIC * (pre * pre * pre)))
    return 0.5 * pre * (1.0 + tangent)


def gelu_pair(pre):
    squared = pre * pre
    tangent = jnp.tanh(GELU_SCALE * (pre + GELU_CUBIC * (squared * pre)))
    half = 0.5 * (1.0 + tangent)
    slopes = half + 0.5 * pre * (1.0 - tangent * tangent) * (
        GELU_SCALE + GELU_SCALE * 3.0 * GELU_CUBIC * squared
    )
    return pre * half, slopes


def flip(values):
    return values.astype(F32).T.astype(BF)


def head_rows(head):
    return pl.ds(pl.multiple_of(head * HEAD_DIM, HEAD_DIM), HEAD_DIM)


def fill_bias(live_column, bias_ref):
    keys = lax.broadcasted_iota(jnp.int32, (PATCH, PATCH), 0)
    queries = lax.broadcasted_iota(jnp.int32, (PATCH, PATCH), 1)
    allowed = (live_column > 0) | (keys == queries)
    bias_ref[...] = jnp.where(allowed, 0.0, -1e30)


def attend(query, key, value, s):
    for head in range(HEADS):
        s.key_heads[head] = key[:, head * HEAD_DIM : (head + 1) * HEAD_DIM]
    s.query_t[...] = (query.astype(F32) * HEAD_DIM ** (-0.5)).T.astype(BF)
    s.value_t[...] = flip(value)

    def one_head(head, carry):
        rows = head_rows(head)
        scores = dot(s.key_heads[head], s.query_t[rows, :])
        weights = jnp.exp(scores + s.bias[...])
        inverse = 1.0 / jnp.sum(weights, axis=0, keepdims=True)
        s.inverse_sum[head] = inverse
        probability = (weights * inverse).astype(BF)
        s.heads_t[rows, :] = dot(s.value_t[rows, :], probability).astype(BF)
        return carry

    lax.fori_loop(0, HEADS, one_head, 0, unroll=2)


def attend_back(key, value, grad_heads, s):
    for head in range(HEADS):
        s.value_heads[head] = value[:, head * HEAD_DIM : (head + 1) * HEAD_DIM]
    s.key_t[...] = flip(key)
    s.grad_heads_t[...] = flip(grad_heads)

    def one_head(head, carry):
        rows = head_rows(head)
        query_rows = s.query_t[rows, :]
        grad_rows = s.grad_heads_t[rows, :]
        scores = dot(s.key_heads[head], query_rows)
        probability = jnp.exp(scores + s.bias[...]) * s.inverse_sum[head]
        grad_wide = grad_rows.astype(F32) * HEAD_DIM ** (-0.5)
        inner = jnp.sum(grad_wide * s.heads_t[rows, :].astype(F32), axis=0, keepdims=True)
        grad_prob = dot(s.value_heads[head], grad_wide.astype(BF))
        grad_score = (probability * (grad_prob - inner)).astype(BF)
        s.grad_value_t[rows, :] = dot(grad_rows, probability.astype(BF), 1, 1).astype(BF)
        s.grad_query_t[rows, :] = dot(s.key_t[rows, :], grad_score).astype(BF)
        s.grad_key_t[rows, :] = (
            dot(query_rows, grad_score, 1, 1) * HEAD_DIM**0.5
        ).astype(BF)
        return carry

    lax.fori_loop(0, HEADS, one_head, 0, unroll=2)


def feed_forward(middle, up_weight, gain_feed):
    normed_m, inverse_m, scaled_m = norm_rows(middle, gain_feed)
    return normed_m, inverse_m, scaled_m, dot(scaled_m, up_weight)


def backward(part, grad_rows, x, middle, key, value, w, s, out, want_grad_in):
    normed_m, inverse_m, scaled_m, pre = feed_forward(middle, w.up[...], w.gain_feed[...])
    activated, slopes = gelu_pair(pre)
    s.hidden[...] = activated.astype(BF)
    s.turned[...] = flip(scaled_m)
    quarter = pl.ds(pl.multiple_of(part * (WIDTH // 4), WIDTH // 4), WIDTH // 4)
    hidden_part = s.hidden[:, pl.ds(pl.multiple_of(part * WIDTH, WIDTH), WIDTH)]
    out[512:768, :] = dot(hidden_part, grad_rows, 0, 0).astype(out.dtype)
    grad_pre = (dot(grad_rows, w.down[...], 1, 1) * slopes).astype(BF)
    up_grad = dot(s.turned[quarter, :], grad_pre)
    for piece in range(4):
        out[256 + 64 * piece : 320 + 64 * piece, :] = up_grad[
            :, WIDTH * piece : WIDTH * (piece + 1)
        ].astype(out.dtype)
    grad_scaled_m = dot(grad_pre, w.up[...], 1, 1)
    feed_gain = jnp.sum(grad_scaled_m * normed_m, axis=0, keepdims=True)
    grad_middle = (
        grad_rows.astype(F32)
        + norm_back(grad_scaled_m, normed_m, inverse_m, w.gain_feed[...])
    ).astype(BF)
    out[192:256, :] = dot(s.heads_t[quarter, :], grad_middle).astype(out.dtype)
    grad_heads = dot(grad_middle, w.out[...], 1, 1).astype(BF)
    attend_back(key, value, grad_heads, s)
    normed_a, inverse_a, scaled_a = norm_rows(x, w.gain_mixer[...])
    s.turned[...] = flip(scaled_a)
    scaled_part = s.turned[quarter, :]
    out[0:64, :] = dot(scaled_part, s.grad_query_t[...], 1, 1).astype(out.dtype)
    out[64:128, :] = dot(scaled_part, s.grad_key_t[...], 1, 1).astype(out.dtype)
    out[128:192, :] = dot(scaled_part, s.grad_value_t[...], 1, 1).astype(out.dtype)
    grad_scaled_a = (
        dot(w.query[...], s.grad_query_t[...])
        + dot(w.key[...], s.grad_key_t[...])
        + dot(w.value[...], s.grad_value_t[...])
    ).T
    mixer_gain = jnp.sum(grad_scaled_a * normed_a, axis=0, keepdims=True)
    gains = jnp.concatenate([mixer_gain, feed_gain, jnp.zeros((14, WIDTH), F32)], axis=0)
    out[768:784, :] = gains.astype(out.dtype)
    out[784:, :] = jnp.zeros((out.shape[0] - 784, WIDTH), out.dtype)
    if not want_grad_in:
        return None
    return (
        grad_middle.astype(F32) + norm_back(grad_scaled_a, normed_a, inverse_a, w.gain_mixer[...])
    ).astype(BF)


class Named:
    def __init__(self, names, refs):
        for name, ref in zip(names, refs, strict=True):
            setattr(self, name, ref)


WEIGHTS = ("gain_mixer", "query", "key", "value", "out", "gain_feed", "up", "down")
FORWARD_SCRATCH = (
    ("key_heads", (HEADS, PATCH, HEAD_DIM), BF),
    ("query_t", (WIDTH, PATCH), BF),
    ("value_t", (WIDTH, PATCH), BF),
    ("bias", (PATCH, PATCH), F32),
    ("inverse_sum", (HEADS, 1, PATCH), F32),
    ("heads_t", (WIDTH, PATCH), BF),
)
BACKWARD_SCRATCH = (
    ("value_heads", (HEADS, PATCH, HEAD_DIM), BF),
    ("key_t", (WIDTH, PATCH), BF),
    ("grad_heads_t", (WIDTH, PATCH), BF),
    ("grad_query_t", (WIDTH, PATCH), BF),
    ("grad_key_t", (WIDTH, PATCH), BF),
    ("grad_value_t", (WIDTH, PATCH), BF),
    ("turned", (WIDTH, PATCH), BF),
    ("hidden", (PATCH, HIDDEN), BF),
)


def project(scaled, w, s):
    query = dot(scaled, w.query[...]).astype(BF)
    key = dot(scaled, w.key[...]).astype(BF)
    value = dot(scaled, w.value[...]).astype(BF)
    return query, key, value


def forward(x, live_column, w, s):
    fill_bias(live_column, s.bias)
    normed, inverse, scaled = norm_rows(x, w.gain_mixer[...])
    query, key, value = project(scaled, w, s)
    attend(query, key, value, s)
    heads_out = s.heads_t[...].astype(F32).T.astype(BF)
    middle = (x.astype(F32) + dot(heads_out, w.out[...])).astype(BF)
    return key, value, middle


def first_kernel(*refs):
    count_ref, x_ref, depart_ref = refs[:3]
    w = Named(WEIGHTS, refs[3:11])
    packed_ref, key_ref, value_ref, middle_ref, query_t_ref, heads_t_ref, inverse_ref = refs[11:18]
    s = Named(("key_heads", "value_t", "bias"), refs[18:21])
    s.query_t = query_t_ref
    s.heads_t = heads_t_ref
    s.inverse_sum = inverse_ref
    x = x_ref[...]
    live = (lax.broadcasted_iota(jnp.int32, (PATCH, 1), 0) < count_ref[0]).astype(jnp.int32)
    key, value, middle = forward(x, live, w, s)
    key_ref[...] = key
    value_ref[...] = value
    middle_ref[...] = middle
    _, _, _, pre = feed_forward(middle, w.up[...], w.gain_feed[...])
    block_out = (middle.astype(F32) + dot(gelu(pre).astype(BF), w.down[...])).astype(BF)
    places = lax.broadcasted_iota(jnp.int32, (packed_ref.shape[0], PATCH), 0)
    chosen = (places == depart_ref[...]).astype(BF)
    packed_ref[...] = dot(chosen, block_out).astype(BF)


def middle_kernel(*refs):
    part_ref, arrived_ref, live_ref, arrive_row_ref, arrive_column_ref, cotangent_ref = refs[:6]
    w = Named(WEIGHTS, refs[6:14])
    out_ref, grads_ref, packed_ref = refs[14:17]
    s = Named([name for name, _, _ in FORWARD_SCRATCH + BACKWARD_SCRATCH], refs[17:31])
    rows_ref = refs[31]
    part = part_ref[0]
    buffer_rows = arrived_ref.shape[0]
    columns = lax.broadcasted_iota(jnp.int32, (PATCH, buffer_rows), 1)
    chosen = (columns == arrive_column_ref[...]).astype(BF)
    x = dot(chosen, arrived_ref[...]).astype(BF)
    key, value, middle = forward(x, live_ref[...], w, s)
    own = pl.ds(pl.multiple_of(part * (PATCH // 4), PATCH // 4), PATCH // 4)
    rows_ref[...] = middle
    middle_part = rows_ref[own, :]
    _, _, _, pre = feed_forward(middle_part, w.up[...], w.gain_feed[...])
    out_ref[...] = (
        middle_part.astype(F32) + dot(gelu(pre).astype(BF), w.down[...])
    ).astype(BF)
    grad_in = backward(
        part, cotangent_ref[...], x, middle, key, value, w, s, grads_ref, True
    )
    places = lax.broadcasted_iota(jnp.int32, (buffer_rows, PATCH), 0)
    packed_ref[...] = dot((places == arrive_row_ref[...]).astype(BF), grad_in).astype(BF)


def last_kernel(*refs):
    part_ref, count_ref, arrived_ref, depart_column_ref, x_ref = refs[:5]
    key_ref, value_ref, middle_ref, query_t_ref, heads_t_ref, inverse_ref = refs[5:11]
    w = Named(WEIGHTS, refs[11:19])
    grads_ref = refs[19]
    s = Named(
        [name for name, _, _ in FORWARD_SCRATCH[:1] + FORWARD_SCRATCH[3:4] + BACKWARD_SCRATCH],
        refs[20:30],
    )
    s.query_t = query_t_ref
    s.heads_t = heads_t_ref
    s.inverse_sum = inverse_ref
    live = (lax.broadcasted_iota(jnp.int32, (PATCH, 1), 0) < count_ref[0]).astype(jnp.int32)
    fill_bias(live, s.bias)
    columns = lax.broadcasted_iota(jnp.int32, (PATCH, arrived_ref.shape[0]), 1)
    chosen = (columns == depart_column_ref[...]).astype(BF)
    grad_rows = dot(chosen, arrived_ref[...]).astype(BF)
    key = key_ref[...]
    for head in range(HEADS):
        s.key_heads[head] = key[:, head * HEAD_DIM : (head + 1) * HEAD_DIM]
    backward(
        part_ref[0], grad_rows, x_ref[...], middle_ref[...], key, value_ref[...], w, s,
        grads_ref, False,
    )


def whole(array):
    zeros = (0,) * array.ndim
    return pl.BlockSpec(array.shape, lambda step: zeros)


def weight_spec(array, block):
    zeros = (0,) * (array.ndim - 1)
    return pl.BlockSpec((None,) + array.shape[1:], lambda step: (block,) + zeros)


def call(kernel, scalars, arrays, weights, block, out_shapes, scratch, name):
    return pl.pallas_call(
        kernel,
        grid=(1,),
        out_shape=out_shapes,
        in_specs=[pl.BlockSpec(memory_space=pltpu.SMEM) for _ in scalars]
        + [whole(array) for array in arrays]
        + [weight_spec(array, block) for array in weights],
        out_specs=jax.tree.map(whole, out_shapes),
        scratch_shapes=[pltpu.VMEM(shape, dtype) for _, shape, dtype in scratch],
        compiler_params=pltpu.CompilerParams(vmem_limit_bytes=56 * 1024 * 1024),
        name=name,
    )(*scalars, *arrays, *weights)


def exchange(buffer):
    return lax.all_to_all(buffer, "patch", split_axis=0, concat_axis=0, tiled=True)


def fold(terms):
    shaped = terms.reshape(terms.shape[0] // SLOTS, SLOTS, WIDTH)
    return jnp.sum(shaped.astype(F32), axis=0).astype(BF)


def body(
    points,
    patch_counts,
    to_hilbert,
    from_hilbert,
    cotangent,
    gain_mixer,
    query_weight,
    key_weight,
    value_weight,
    out_weight,
    gain_feed,
    up_weight,
    down_weight,
):
    peer_count = lax.axis_size("patch")
    buffer_rows = peer_count * SLOTS
    part = lax.axis_index("mp").astype(jnp.int32).reshape(1)
    count = lax.dynamic_slice_in_dim(patch_counts, lax.axis_index("patch"), 1, 0)
    position = jnp.arange(PATCH, dtype=jnp.int32)

    def places(owners, ranking):
        ahead = (owners[:, None] == owners[None, :]) & (ranking[None, :] < ranking[:, None])
        return owners * SLOTS + jnp.sum(ahead.astype(jnp.int32), axis=1)

    depart = places(to_hilbert // PATCH, position)
    arrive = places(from_hilbert // PATCH, from_hilbert)
    source_patch = from_hilbert // PATCH
    source_count = jnp.sum(
        jnp.where(
            source_patch[:, None] == jnp.arange(peer_count, dtype=jnp.int32)[None, :],
            patch_counts[None, :],
            0,
        ),
        axis=1,
    )
    live_hilbert = (from_hilbert % PATCH < source_count).astype(jnp.int32)
    weights = (
        gain_mixer[:, None, :],
        query_weight,
        key_weight,
        value_weight,
        out_weight,
        gain_feed[:, None, :],
        up_weight,
        down_weight,
    )
    rows = jax.ShapeDtypeStruct((PATCH, WIDTH), BF)
    turned = jax.ShapeDtypeStruct((WIDTH, PATCH), BF)
    packed = jax.ShapeDtypeStruct((buffer_rows, WIDTH), BF)
    x = lax.all_gather(points, "mp", axis=0, tiled=True)
    cotangent_rows = lax.all_gather(cotangent, "mp", axis=0, tiled=True)
    sent, key, value, middle, query_t, heads_t, inverse = call(
        first_kernel,
        (count,),
        (x, depart[None, :]),
        weights,
        0,
        (
            packed,
            rows,
            rows,
            rows,
            turned,
            turned,
            jax.ShapeDtypeStruct((HEADS, 1, PATCH), F32),
        ),
        (FORWARD_SCRATCH[0], FORWARD_SCRATCH[2], FORWARD_SCRATCH[3]),
        "first_block",
    )
    arrived = exchange(sent)
    hilbert_out, second_grads, grad_sent = call(
        middle_kernel,
        (part,),
        (arrived, live_hilbert[:, None], arrive[None, :], arrive[:, None], cotangent_rows),
        weights,
        1,
        (jax.ShapeDtypeStruct((PATCH // 4, WIDTH), BF), packed, packed),
        FORWARD_SCRATCH + BACKWARD_SCRATCH + (("rows", (PATCH, WIDTH), BF),),
        "second_block",
    )
    grad_arrived = exchange(grad_sent)
    first_grads = call(
        last_kernel,
        (part, count),
        (grad_arrived, depart[:, None], x, key, value, middle, query_t, heads_t, inverse),
        weights,
        0,
        packed,
        (FORWARD_SCRATCH[0], FORWARD_SCRATCH[3]) + BACKWARD_SCRATCH,
        "first_block_back",
    )
    second_terms = exchange(second_grads)
    first_terms = exchange(first_grads)
    own_sums = jnp.concatenate([fold(first_terms), fold(second_terms)], axis=0)
    spread = jnp.broadcast_to(own_sums[None], (peer_count,) + own_sums.shape)
    both = lax.all_to_all(spread, "patch", split_axis=0, concat_axis=0, tiled=True)
    both = both.reshape(peer_count, 2, SLOTS, WIDTH).transpose(1, 0, 2, 3)
    both = both.reshape(2, buffer_rows, WIDTH).astype(F32)
    up_grad = both[:, 256:512].reshape(2, 4, 64, WIDTH).transpose(0, 2, 1, 3).reshape(2, 64, HIDDEN)
    return (
        hilbert_out,
        both[:, 768],
        both[:, 0:64],
        both[:, 64:128],
        both[:, 128:192],
        both[:, 192:256],
        both[:, 769],
        up_grad,
        both[:, 512:768],
    )


def solution(mesh):
    split = P(("patch", "mp"), None)
    in_specs = (split, P(), P("patch"), P("patch"), split) + (P(),) * 8
    own_rows = P(None, "mp", None)
    out_specs = (split, P(), own_rows, own_rows, own_rows, own_rows, P(), own_rows, own_rows)
    return jax.shard_map(body, mesh=mesh, in_specs=in_specs, out_specs=out_specs, check_vma=False)
```

```python
import functools

import jax
import jax.numpy as jnp
from jax import lax
from jax.experimental import pallas as pl
from jax.experimental.pallas import tpu as pltpu
from jax.sharding import PartitionSpec as P

HEADS = 16
PATCH = 512
HEAD_DIM = 16
WIDTH = 256
HIDDEN = 1024
SLOTS = 8
VALUE_SCALE = 1024.0
ALLOWED = -0.0078125
LANES = 128
WEIGHT_ROWS = 768
HALF_ROWS = WEIGHT_ROWS + 16

EPSILON = 1e-05
GELU_SCALE = 0.7978845608028654
GELU_CUBIC = 0.044715

BF = jnp.bfloat16
F32 = jnp.float32


def dot(left, right, left_dim=1, right_dim=0):
    return lax.dot_general(
        left, right, (((left_dim,), (right_dim,)), ((), ())), preferred_element_type=F32
    )


def norm_rows(values, gain_row):
    widened = values.astype(F32)
    centered = widened - jnp.mean(widened, axis=1, keepdims=True)
    inverse = lax.rsqrt(jnp.mean(centered * centered, axis=1, keepdims=True) + EPSILON)
    normed = centered * inverse
    return normed, inverse, (normed * gain_row).astype(BF)


def norm_back(grad_scaled, normed, inverse, gain_row):
    grad_normed = grad_scaled * gain_row
    centered = grad_normed - jnp.mean(grad_normed, axis=1, keepdims=True)
    return inverse * (centered - normed * jnp.mean(grad_normed * normed, axis=1, keepdims=True))


def gelu(pre):
    tangent = jnp.tanh(GELU_SCALE * (pre + GELU_CUBIC * (pre * pre * pre)))
    return 0.5 * pre * (1.0 + tangent)


def gelu_pair(pre):
    squared = pre * pre
    tangent = jnp.tanh(GELU_SCALE * (pre + GELU_CUBIC * (squared * pre)))
    half = 0.5 * (1.0 + tangent)
    slopes = half + 0.5 * pre * (1.0 - tangent * tangent) * (
        GELU_SCALE + GELU_SCALE * 3.0 * GELU_CUBIC * squared
    )
    return pre * half, slopes


def flip(values):
    return values.astype(F32).T.astype(BF)


def head_rows(head):
    return slice(head * HEAD_DIM, (head + 1) * HEAD_DIM)


def fill_bias(live_column, bias_ref):
    keys = lax.broadcasted_iota(jnp.int32, (PATCH, PATCH), 0)
    queries = lax.broadcasted_iota(jnp.int32, (PATCH, PATCH), 1)
    allowed = (live_column > 0) | (keys == queries)
    bias_ref[...] = jnp.where(allowed, ALLOWED, -1e30)


def attend(query, key, value, s, after_head=None):
    s.query_t[...] = (query.astype(F32) * HEAD_DIM ** (-0.5)).T.astype(BF)
    s.value_t[...] = (value.astype(F32) * (1.0 / VALUE_SCALE)).T.astype(BF)

    for head in range(HEADS):
        rows = head_rows(head)
        weights = jnp.exp(dot(key[:, rows], s.query_t[rows, :]) + s.bias[...])
        inverse = 1.0 / jnp.sum(weights, axis=0, keepdims=True)
        s.inverse_sum[head] = inverse
        lowered = weights.astype(BF)
        s.weights[head] = lowered
        if after_head is not None:
            after_head(head)
        mixed = dot(s.value_t[rows, :], lowered)
        s.heads_t[rows, :] = (mixed * (inverse * VALUE_SCALE)).astype(BF)


def attend_back(key, value, grad_heads, s):
    s.key_t[...] = flip(key)
    s.grad_heads_t[...] = flip(grad_heads)
    query_t, heads_t, inverse_sum, weights = s.query_t, s.heads_t, s.inverse_sum, s.weights

    for head in range(HEADS):
        rows = head_rows(head)
        query_rows = query_t[rows, :]
        grad_rows = s.grad_heads_t[rows, :]
        probability = weights[head].astype(F32) * inverse_sum[head]
        grad_wide = grad_rows.astype(F32) * HEAD_DIM ** (-0.5)
        inner = jnp.sum(grad_wide * heads_t[rows, :].astype(F32), axis=0, keepdims=True)
        grad_prob = dot(value[:, rows], grad_wide.astype(BF))
        grad_score = (probability * (grad_prob - inner)).astype(BF)
        s.grad_value_t[rows, :] = dot(grad_rows, probability.astype(BF), 1, 1).astype(BF)
        s.grad_query_t[rows, :] = dot(s.key_t[rows, :], grad_score).astype(BF)
        s.grad_key_t[rows, :] = (
            dot(query_rows, grad_score, 1, 1) * HEAD_DIM**0.5
        ).astype(BF)


def feed_forward(middle, up_weight, gain_feed):
    normed_m, inverse_m, scaled_m = norm_rows(middle, gain_feed)
    return normed_m, inverse_m, scaled_m, dot(scaled_m, up_weight)


def backward(part, core, grad_rows, x, middle, key, value, w, s, halves, want_grad_in):
    def put(first_row, grad):
        rows = slice(first_row, first_row + grad.shape[0])
        low, high = grad[:, :LANES], grad[:, LANES:]
        halves[0][rows, :] = jnp.where(core == 0, low, high).astype(halves[0].dtype)
        halves[1][rows, :] = jnp.where(core == 0, high, low).astype(halves[1].dtype)

    normed_m, inverse_m, scaled_m, pre = feed_forward(middle, w.up[...], w.gain_feed)
    activated, slopes = gelu_pair(pre)
    s.hidden[...] = activated.astype(BF)
    s.turned[...] = flip(scaled_m)
    quarter = pl.ds(pl.multiple_of(part * (WIDTH // 4), WIDTH // 4), WIDTH // 4)
    hidden_part = s.hidden[:, pl.ds(pl.multiple_of(part * WIDTH, WIDTH), WIDTH)]
    put(512, dot(hidden_part, grad_rows, 0, 0))
    grad_pre = (dot(grad_rows, w.down[...], 1, 1) * slopes).astype(BF)
    up_grad = dot(s.turned[quarter, :], grad_pre)
    for piece in range(4):
        put(256 + 64 * piece, up_grad[:, WIDTH * piece : WIDTH * (piece + 1)])
    grad_scaled_m = dot(grad_pre, w.up[...], 1, 1)
    feed_gain = jnp.sum(grad_scaled_m * normed_m, axis=0, keepdims=True)
    grad_middle = (
        grad_rows.astype(F32)
        + norm_back(grad_scaled_m, normed_m, inverse_m, w.gain_feed)
    ).astype(BF)
    put(192, dot(s.heads_t[quarter, :], grad_middle))
    grad_heads = dot(grad_middle, w.out[...], 1, 1).astype(BF)
    attend_back(key[...], value[...], grad_heads, s)
    normed_a, inverse_a, scaled_a = norm_rows(x[...].reshape(PATCH, WIDTH), w.gain_mixer)
    s.turned[...] = flip(scaled_a)
    scaled_part = s.turned[quarter, :]
    put(0, dot(scaled_part, s.grad_query_t[...], 1, 1))
    put(64, dot(scaled_part, s.grad_key_t[...], 1, 1))
    put(128, dot(scaled_part, s.grad_value_t[...], 1, 1))
    grad_scaled_a = (
        dot(w.query[...], s.grad_query_t[...])
        + dot(w.key[...], s.grad_key_t[...])
        + dot(w.value[...], s.grad_value_t[...])
    ).T
    mixer_gain = jnp.sum(grad_scaled_a * normed_a, axis=0, keepdims=True)
    gains = jnp.concatenate([mixer_gain, feed_gain, jnp.zeros((14, WIDTH), F32)], axis=0)
    put(WEIGHT_ROWS, gains)
    if not want_grad_in:
        return None
    return (
        grad_middle.astype(F32) + norm_back(grad_scaled_a, normed_a, inverse_a, w.gain_mixer)
    ).astype(BF)


class Inputs:
    def __init__(self, names, sources, buffers, sems, block, early):
        self.block, self.copies = block, {}
        self.buffers = dict(zip(names, buffers, strict=True))
        for place, (name, source) in enumerate(zip(names, sources, strict=True)):
            self.copies[name] = pltpu.make_async_copy(source, self.buffers[name], sems.at[place])
        self.rest = list(self.copies.values())[early:]
        for copy in list(self.copies.values())[:early]:
            copy.start()

    def wait(self, *names):
        for name in names:
            if name in self.copies:
                self.copies.pop(name).wait()

    def start_rest(self):
        for copy in self.rest:
            copy.start()
        self.rest = []

    def __getattr__(self, name):
        if name not in self.__dict__.get("buffers", ()):
            raise AttributeError(name)
        self.wait(name)
        if name in GAINS:
            return self.buffers[name][self.block : self.block + 1, :]
        return self.buffers[name]


class Scratch:
    def __init__(self, names, refs, inputs=None):
        self.inputs = inputs
        for name, ref in zip(names, refs, strict=True):
            setattr(self, name, ref)

    def __getattr__(self, name):
        return getattr(self.__dict__["inputs"], name)


def as_column(row):
    wide = jnp.broadcast_to(row.astype(F32), (8, row.shape[1]))
    return wide.T[:, :1].astype(jnp.int32)


GAINS = ("gain_mixer", "gain_feed")
WEIGHTS = ("gain_mixer", "query", "key", "value", "out", "gain_feed", "up", "down")
FORWARD_SCRATCH = (
    ("query_t", (WIDTH, PATCH), BF),
    ("value_t", (WIDTH, PATCH), BF),
    ("bias", (PATCH, PATCH), F32),
    ("weights", (HEADS, PATCH, PATCH), BF),
    ("inverse_sum", (HEADS, 1, PATCH), F32),
    ("heads_t", (WIDTH, PATCH), BF),
)
BACKWARD_SCRATCH = (
    ("key_t", (WIDTH, PATCH), BF),
    ("grad_heads_t", (WIDTH, PATCH), BF),
    ("grad_query_t", (WIDTH, PATCH), BF),
    ("grad_key_t", (WIDTH, PATCH), BF),
    ("grad_value_t", (WIDTH, PATCH), BF),
    ("turned", (WIDTH, PATCH), BF),
    ("hidden", (PATCH, HIDDEN), BF),
)


SCRATCH = {name: (shape, dtype) for name, shape, dtype in FORWARD_SCRATCH + BACKWARD_SCRATCH}
VMEM_BYTES = 58 * 1024 * 1024


def project(scaled, w):
    query = dot(scaled, w.query[...]).astype(BF)
    key = dot(scaled, w.key[...]).astype(BF)
    value = dot(scaled, w.value[...]).astype(BF)
    return query, key, value


def forward(x, live_column, w, s, after_head=None):
    fill_bias(live_column, s.bias)
    normed, inverse, scaled = norm_rows(x, w.gain_mixer)
    query, key, value = project(scaled, w)
    w.start_rest()
    attend(query, key, value, s, after_head)
    heads_out = s.heads_t[...].astype(F32).T.astype(BF)
    middle = (x.astype(F32) + dot(heads_out, w.out[...])).astype(BF)
    return key, value, middle


def own_live(count):
    return (lax.broadcasted_iota(jnp.int32, (PATCH, 1), 0) < count).astype(jnp.int32)


def first_kernel(w, outs, scratch):
    packed_ref, key_ref, value_ref, middle_ref, query_t_ref, heads_t_ref, inverse_ref = outs[:7]
    sems = scratch[-1]
    s = Scratch(("value_t", "bias", "weights"), scratch[:-1])
    s.query_t = query_t_ref
    s.heads_t = heads_t_ref
    s.inverse_sum = inverse_ref

    def kept_copy(head):
        return pltpu.make_async_copy(s.weights.at[head], outs[7].at[head], sems.at[head])

    live = own_live(w.counts[lax.axis_index("patch")])
    x = w.rows[...].reshape(PATCH, WIDTH)
    key, value, middle = forward(x, live, w, s, lambda head: kept_copy(head).start())
    key_ref[...] = key
    value_ref[...] = value
    middle_ref[...] = middle
    _, _, _, pre = feed_forward(middle, w.up[...], w.gain_feed)
    block_out = (middle.astype(F32) + dot(gelu(pre).astype(BF), w.down[...])).astype(BF)
    places = lax.broadcasted_iota(jnp.int32, (packed_ref.shape[0], PATCH), 0)
    chosen = (places == w.depart[...]).astype(BF)
    packed_ref[...] = dot(chosen, block_out).astype(BF)

    def finish_copy(head, carry):
        kept_copy(head).wait()
        return carry

    lax.fori_loop(0, HEADS, finish_copy, 0)


def unpack(arrived, places):
    columns = lax.broadcasted_iota(jnp.int32, (PATCH, arrived.shape[0]), 1)
    chosen = (columns == as_column(places[...])).astype(BF)
    return dot(chosen, arrived[...]).astype(BF)


def second_kernel(w, outs, scratch):
    out_ref, keep_ref, give_ref, packed_ref = outs
    s = Scratch(SCRATCH, scratch[:-1])
    rows_ref = scratch[-1]
    part = lax.axis_index("mp")
    core = lax.rem(lax.axis_index("patch"), 2)
    x = unpack(w.arrived, w.arrive)
    key, value, middle = forward(x, as_column(w.live[...]), w, s)
    own = pl.ds(pl.multiple_of(part * (PATCH // 4), PATCH // 4), PATCH // 4)
    rows_ref[...] = middle
    middle_part = rows_ref[own, :]
    _, _, _, pre = feed_forward(middle_part, w.up[...], w.gain_feed)
    out_ref[...] = (
        middle_part.astype(F32) + dot(gelu(pre).astype(BF), w.down[...])
    ).astype(BF)
    cotangent = w.cotangent[...].reshape(PATCH, WIDTH)
    grad_in = backward(
        part, core, cotangent, x, middle, key, value, w, s, (keep_ref, give_ref), True
    )
    places = lax.broadcasted_iota(jnp.int32, (packed_ref.shape[0], PATCH), 0)
    packed_ref[...] = dot((places == w.arrive[...]).astype(BF), grad_in).astype(BF)


def last_kernel(w, outs, scratch):
    s = Scratch([name for name, _, _ in BACKWARD_SCRATCH], scratch[:-2], w)
    halves = scratch[-2:]
    w.start_rest()
    grad_rows = unpack(w.arrived, w.depart)
    middle = w.middle[...]
    backward(
        lax.axis_index("mp"), lax.rem(lax.axis_index("patch"), 2), grad_rows, w.rows, middle,
        w.key_rows, w.value_rows, w, s, halves, False,
    )
    chips = outs[0].shape[0]
    for out_ref, half, second in zip(outs, halves, (w.second_keep, w.second_give), strict=True):
        second = second[...].astype(F32)
        rows = jnp.concatenate([half[:WEIGHT_ROWS, :], second[:WEIGHT_ROWS, :]], axis=0)
        gains = jnp.concatenate(
            [
                half[WEIGHT_ROWS : WEIGHT_ROWS + 2, :],
                second[WEIGHT_ROWS : WEIGHT_ROWS + 2, :],
                jnp.zeros((4, LANES), F32),
            ],
            axis=0,
        )
        out_ref[...] = jnp.concatenate(
            [
                rows.reshape(chips, rows.shape[0] // chips, LANES),
                jnp.broadcast_to(gains[None], (chips, 8, LANES)),
            ],
            axis=1,
        ).astype(BF)


def finish_kernel(w, outs, scratch):
    mixer_ref, query_ref, key_ref, value_ref, out_ref, feed_ref, up_ref, down_ref = outs
    own_ref, other_ref = w.own, w.other
    core = lax.rem(lax.axis_index("patch"), 2)
    share = 2 * WEIGHT_ROWS // own_ref.shape[0]
    own_rows = own_ref[...].astype(F32)[:, :share, :].reshape(2 * WEIGHT_ROWS, LANES)
    other_rows = other_ref[...].astype(F32)[:, :share, :].reshape(2 * WEIGHT_ROWS, LANES)

    def join(own, other):
        low = jnp.where(core == 0, own, other)
        return jnp.concatenate([low, jnp.where(core == 0, other, own)], axis=1)

    gains = join(own_ref[0].astype(F32)[share:, :], other_ref[0].astype(F32)[share:, :])
    for block in range(2):

        def rows(first, size):
            there = slice(WEIGHT_ROWS * block + first, WEIGHT_ROWS * block + first + size)
            return join(own_rows[there, :], other_rows[there, :])

        for place, ref in enumerate((query_ref, key_ref, value_ref, out_ref)):
            ref[block] = rows(64 * place, 64)
        for piece in range(4):
            up_ref[block, :, WIDTH * piece : WIDTH * (piece + 1)] = rows(256 + 64 * piece, 64)
        down_ref[block] = rows(512, 256)
        mixer_ref[block : block + 1, :] = gains[2 * block : 2 * block + 1, :]
        feed_ref[block : block + 1, :] = gains[2 * block + 1 : 2 * block + 2, :]


def whole(array):
    zeros = (0,) * len(array.shape)
    return pl.BlockSpec(array.shape, lambda step: zeros)


HBM = pl.BlockSpec(memory_space=pltpu.HBM)


def call(kernel, inputs, weights, block, early, outputs, scratch, name):
    inputs = [(name, array, part) for name, array, part in inputs]
    inputs += [
        (weight, array, None if weight in GAINS else (block,))
        for weight, array in zip(WEIGHTS, weights)
    ]
    inputs.sort(key=lambda entry: early.index(entry[0]) if entry[0] in early else len(early))
    names = [name for name, _, _ in inputs]
    parts = [part for _, _, part in inputs]
    arrays = [array for _, array, _ in inputs]
    shapes = [
        jax.eval_shape(lambda a, part=part: a if part is None else a[part], array)
        for array, part in zip(arrays, parts)
    ]
    buffers = [
        pltpu.SMEM(shape.shape, shape.dtype)
        if name == "counts"
        else pltpu.VMEM(shape.shape, shape.dtype)
        for name, shape in zip(names, shapes)
    ]
    first_out, first_scratch = len(arrays), len(arrays) + len(outputs)
    first_buffer = first_scratch + len(scratch)

    def whole_kernel(*refs):
        sources = [
            ref if part is None else ref.at[part] for ref, part in zip(refs[:first_out], parts)
        ]
        taken = Inputs(names, sources, refs[first_buffer:-1], refs[-1], block, len(early))
        kernel(taken, refs[first_out:first_scratch], refs[first_scratch:first_buffer])

    return pl.pallas_call(
        whole_kernel,
        grid=(1,),
        out_shape=[shape for shape, _ in outputs],
        in_specs=[HBM] * len(arrays),
        out_specs=[spec or whole(shape) for shape, spec in outputs],
        scratch_shapes=[*scratch, *buffers, pltpu.SemaphoreType.DMA((len(arrays),))],
        compiler_params=pltpu.CompilerParams(
            vmem_limit_bytes=VMEM_BYTES if weights else VMEM_BYTES // 4
        ),
        name=name,
    )(*arrays)


def vmem(*names):
    return [pltpu.VMEM(SCRATCH[name][0], SCRATCH[name][1]) for name in names]


def first_call(counts, gathered, depart, weights, buffer_rows):
    rows = jax.ShapeDtypeStruct((PATCH, WIDTH), BF)
    turned = jax.ShapeDtypeStruct((WIDTH, PATCH), BF)
    return call(
        first_kernel,
        [("rows", gathered, (slice(None), 0)), ("counts", counts, None), ("depart", depart, None)],
        weights,
        0,
        ("rows", "gain_mixer", "query", "key", "value", "counts"),
        [(jax.ShapeDtypeStruct((buffer_rows, WIDTH), BF), None)]
        + [(rows, None)] * 3
        + [(turned, None)] * 2
        + [
            (jax.ShapeDtypeStruct((HEADS, 1, PATCH), F32), None),
            (jax.ShapeDtypeStruct((HEADS, PATCH, PATCH), BF), HBM),
        ],
        vmem("value_t", "bias", "weights") + [pltpu.SemaphoreType.DMA((HEADS,))],
        "first_block",
    )


def second_call(arrived, live, arrive, gathered, weights):
    half = jax.ShapeDtypeStruct((HALF_ROWS, LANES), BF)
    return call(
        second_kernel,
        [
            ("arrive", arrive, None), ("arrived", arrived, None), ("live", live, None),
            ("cotangent", gathered, (slice(None), 1)),
        ],
        weights,
        1,
        ("arrive", "arrived", "gain_mixer", "query", "key", "value", "live"),
        [
            (jax.ShapeDtypeStruct((PATCH // 4, WIDTH), BF), None), (half, None), (half, None),
            (jax.ShapeDtypeStruct(arrived.shape, BF), None),
        ],
        vmem(*SCRATCH) + [pltpu.VMEM((PATCH, WIDTH), BF)],
        "second_block",
    )


def last_call(arrived, depart, gathered, kept, second, weights, chips):
    key, value, middle, query_t, heads_t, inverse, attention = kept
    terms = jax.ShapeDtypeStruct((chips, 32, LANES), BF)
    return call(
        last_kernel,
        [
            ("depart", depart, None), ("arrived", arrived, None), ("middle", middle, None),
            ("heads_t", heads_t, None), ("rows", gathered, (slice(None), 0)),
            ("key_rows", key, None), ("value_rows", value, None), ("query_t", query_t, None),
            ("inverse_sum", inverse, None), ("second_keep", second[0], None),
            ("second_give", second[1], None), ("weights", attention, None),
        ],
        weights,
        0,
        ("depart", "arrived", "middle", "gain_feed", "up", "down"),
        [(terms, None), (terms, None)],
        vmem(*[name for name, _, _ in BACKWARD_SCRATCH])
        + [pltpu.VMEM((HALF_ROWS, LANES), F32)] * 2,
        "first_block_back",
    )


def finish_call(own, other):
    gain = jax.ShapeDtypeStruct((2, WIDTH), F32)
    small = jax.ShapeDtypeStruct((2, WIDTH // 4, WIDTH), F32)
    up = jax.ShapeDtypeStruct((2, WIDTH // 4, HIDDEN), F32)
    down = jax.ShapeDtypeStruct((2, HIDDEN // 4, WIDTH), F32)
    return call(
        finish_kernel,
        [("own", own, None), ("other", other, None)],
        (),
        0,
        ("own", "other"),
        [(shape, None) for shape in (gain, small, small, small, small, gain, up, down)],
        [],
        "finish",
    )


def exchange(buffer, groups=None):
    return lax.all_to_all(
        buffer, "patch", split_axis=0, concat_axis=0, tiled=True, axis_index_groups=groups
    )


def swap_cores(half, peer_count):
    return lax.ppermute(half, "patch", [(i, i ^ 1) for i in range(peer_count)])


def body(
    points,
    patch_counts,
    to_hilbert,
    from_hilbert,
    cotangent,
    gain_mixer,
    query_weight,
    key_weight,
    value_weight,
    out_weight,
    gain_feed,
    up_weight,
    down_weight,
):
    peer_count = lax.axis_size("patch")
    buffer_rows = peer_count * SLOTS
    position = jnp.arange(PATCH, dtype=jnp.int32)

    def places(owners, ranking):
        ahead = (owners[:, None] == owners[None, :]) & (ranking[None, :] < ranking[:, None])
        return owners * SLOTS + jnp.sum(ahead.astype(jnp.int32), axis=1)

    depart = places(to_hilbert // PATCH, position)
    arrive = places(from_hilbert // PATCH, from_hilbert)
    source_patch = from_hilbert // PATCH
    source_count = jnp.sum(
        jnp.where(
            source_patch[:, None] == jnp.arange(peer_count, dtype=jnp.int32)[None, :],
            patch_counts[None, :],
            0,
        ),
        axis=1,
    )
    live_hilbert = (from_hilbert % PATCH < source_count).astype(jnp.int32)
    weights = (
        gain_mixer,
        query_weight,
        key_weight,
        value_weight,
        out_weight,
        gain_feed,
        up_weight,
        down_weight,
    )
    pair = jnp.stack([points, cotangent])
    pair = jnp.broadcast_to(pair[None], (lax.axis_size("mp"),) + pair.shape)
    gathered = lax.all_to_all(pair, "mp", split_axis=0, concat_axis=0, tiled=True)
    sent, *kept = first_call(patch_counts, gathered, depart[None, :], weights, buffer_rows)
    arrived = exchange(sent)
    hilbert_out, second_keep, second_give, grad_sent = second_call(
        arrived, live_hilbert[None, :], arrive[None, :], gathered, weights
    )
    grad_arrived = exchange(grad_sent)
    chips = peer_count // 2
    keep, give = last_call(
        grad_arrived, depart[None, :], gathered, kept,
        (second_keep, second_give), weights, chips,
    )
    taken = swap_cores(give, peer_count)
    terms = (keep.astype(F32) + taken.astype(F32)).astype(BF)
    groups = [[2 * chip + core for chip in range(chips)] for core in range(2)]
    sums = jnp.sum(exchange(terms, groups).astype(F32), axis=0).astype(BF)
    own = exchange(jnp.broadcast_to(sums[None], (chips,) + sums.shape), groups)
    other = swap_cores(own, peer_count)
    return (hilbert_out, *finish_call(own, other))


def solution(mesh):
    split = P(("patch", "mp"), None)
    in_specs = (split, P(), P("patch"), P("patch"), split) + (P(),) * 8
    own_rows = P(None, "mp", None)
    out_specs = (split, P(), own_rows, own_rows, own_rows, own_rows, P(), own_rows, own_rows)
    return jax.shard_map(body, mesh=mesh, in_specs=in_specs, out_specs=out_specs, check_vma=False)
```

```python
import functools

import jax
import jax.numpy as jnp
from jax import lax
from jax.experimental import pallas as pl
from jax.experimental.pallas import tpu as pltpu
from jax.sharding import PartitionSpec as P

HEADS = 16
PATCH = 512
HEAD_DIM = 16
WIDTH = 256
HIDDEN = 1024
SLOTS = 6
PIECES = 1
VALUE_SCALE = 1024.0
ALLOWED = -0.0078125
LANES = 128
WEIGHT_ROWS = 768
HALF_ROWS = WEIGHT_ROWS + 16

EPSILON = 1e-05
GELU_SCALE = 0.7978845608028654
GELU_CUBIC = 0.044715

BF = jnp.bfloat16
F32 = jnp.float32


def dot(left, right, left_dim=1, right_dim=0):
    return lax.dot_general(
        left, right, (((left_dim,), (right_dim,)), ((), ())), preferred_element_type=F32
    )


def norm_rows(values, gain_row):
    widened = values.astype(F32)
    centered = widened - jnp.mean(widened, axis=1, keepdims=True)
    inverse = lax.rsqrt(jnp.mean(centered * centered, axis=1, keepdims=True) + EPSILON)
    normed = centered * inverse
    return normed, inverse, (normed * gain_row).astype(BF)


def norm_back(grad_scaled, normed, inverse, gain_row):
    grad_normed = grad_scaled * gain_row
    centered = grad_normed - jnp.mean(grad_normed, axis=1, keepdims=True)
    return inverse * (centered - normed * jnp.mean(grad_normed * normed, axis=1, keepdims=True))


def gelu(pre):
    tangent = jnp.tanh(GELU_SCALE * (pre + GELU_CUBIC * (pre * pre * pre)))
    return 0.5 * pre * (1.0 + tangent)


def gelu_pair(pre):
    squared = pre * pre
    tangent = jnp.tanh(GELU_SCALE * (pre + GELU_CUBIC * (squared * pre)))
    half = 0.5 * (1.0 + tangent)
    slopes = half + 0.5 * pre * (1.0 - tangent * tangent) * (
        GELU_SCALE + GELU_SCALE * 3.0 * GELU_CUBIC * squared
    )
    return pre * half, slopes


def flip(values):
    return values.astype(F32).T.astype(BF)


def head_rows(head):
    return slice(head * HEAD_DIM, (head + 1) * HEAD_DIM)


def fill_bias(live_column, bias_ref):
    keys = lax.broadcasted_iota(jnp.int32, (PATCH, PATCH), 0)
    queries = lax.broadcasted_iota(jnp.int32, (PATCH, PATCH), 1)
    allowed = (live_column > 0) | (keys == queries)
    bias_ref[...] = jnp.where(allowed, ALLOWED, -1e30)


def attend(query, key, value, s, after_head=None):
    s.query_t[...] = (query.astype(F32) * HEAD_DIM ** (-0.5)).T.astype(BF)
    s.value_t[...] = (value.astype(F32) * (1.0 / VALUE_SCALE)).T.astype(BF)

    for head in range(HEADS):
        rows = head_rows(head)
        weights = jnp.exp(dot(key[:, rows], s.query_t[rows, :]) + s.bias[...])
        inverse = 1.0 / jnp.sum(weights, axis=0, keepdims=True)
        s.inverse_sum[head] = inverse
        lowered = weights.astype(BF)
        s.weights[head] = lowered
        if after_head is not None:
            after_head(head)
        mixed = dot(s.value_t[rows, :], lowered)
        s.heads_t[rows, :] = (mixed * (inverse * VALUE_SCALE)).astype(BF)


def attend_back(key, value, grad_heads, s):
    s.key_t[...] = flip(key)
    s.grad_heads_t[...] = flip(grad_heads)
    query_t, heads_t, inverse_sum = s.query_t, s.heads_t, s.inverse_sum

    for head in range(HEADS):
        rows = head_rows(head)
        query_rows = query_t[rows, :]
        grad_rows = s.grad_heads_t[rows, :]
        probability = s.kept_weights(head).astype(F32) * inverse_sum[head]
        grad_wide = grad_rows.astype(F32) * HEAD_DIM ** (-0.5)
        inner = jnp.sum(grad_wide * heads_t[rows, :].astype(F32), axis=0, keepdims=True)
        grad_prob = dot(value[:, rows], grad_wide.astype(BF))
        grad_score = (probability * (grad_prob - inner)).astype(BF)
        s.grad_value_t[rows, :] = dot(grad_rows, probability.astype(BF), 1, 1).astype(BF)
        s.grad_query_t[rows, :] = dot(s.key_t[rows, :], grad_score).astype(BF)
        s.grad_key_t[rows, :] = (
            dot(query_rows, grad_score, 1, 1) * HEAD_DIM**0.5
        ).astype(BF)


def feed_forward(middle, up_weight, gain_feed):
    normed_m, inverse_m, scaled_m = norm_rows(middle, gain_feed)
    return normed_m, inverse_m, scaled_m, dot(scaled_m, up_weight)


def backward(part, core, grad_rows, x, middle, key, value, w, s, halves, want_grad_in):
    def put(first_row, grad):
        rows = slice(first_row, first_row + grad.shape[0])
        low, high = grad[:, :LANES], grad[:, LANES:]
        halves[0][rows, :] = jnp.where(core == 0, low, high).astype(halves[0].dtype)
        halves[1][rows, :] = jnp.where(core == 0, high, low).astype(halves[1].dtype)

    normed_m, inverse_m, scaled_m, pre = feed_forward(middle, w.up[...], w.gain_feed)
    activated, slopes = gelu_pair(pre)
    s.hidden[...] = activated.astype(BF)
    s.turned[...] = flip(scaled_m)
    quarter = pl.ds(pl.multiple_of(part * (WIDTH // 4), WIDTH // 4), WIDTH // 4)
    hidden_part = s.hidden[:, pl.ds(pl.multiple_of(part * WIDTH, WIDTH), WIDTH)]
    put(512, dot(hidden_part, grad_rows, 0, 0))
    grad_pre = (dot(grad_rows, w.down[...], 1, 1) * slopes).astype(BF)
    up_grad = dot(s.turned[quarter, :], grad_pre)
    for piece in range(4):
        put(256 + 64 * piece, up_grad[:, WIDTH * piece : WIDTH * (piece + 1)])
    grad_scaled_m = dot(grad_pre, w.up[...], 1, 1)
    feed_gain = jnp.sum(grad_scaled_m * normed_m, axis=0, keepdims=True)
    grad_middle = (
        grad_rows.astype(F32)
        + norm_back(grad_scaled_m, normed_m, inverse_m, w.gain_feed)
    ).astype(BF)
    put(192, dot(s.heads_t[quarter, :], grad_middle))
    grad_heads = dot(grad_middle, w.out[...], 1, 1).astype(BF)
    attend_back(key[...], value[...], grad_heads, s)
    normed_a, inverse_a, scaled_a = norm_rows(x[...].reshape(PATCH, WIDTH), w.gain_mixer)
    s.turned[...] = flip(scaled_a)
    scaled_part = s.turned[quarter, :]
    put(0, dot(scaled_part, s.grad_query_t[...], 1, 1))
    put(64, dot(scaled_part, s.grad_key_t[...], 1, 1))
    put(128, dot(scaled_part, s.grad_value_t[...], 1, 1))
    grad_scaled_a = (
        dot(w.query[...], s.grad_query_t[...])
        + dot(w.key[...], s.grad_key_t[...])
        + dot(w.value[...], s.grad_value_t[...])
    ).T
    mixer_gain = jnp.sum(grad_scaled_a * normed_a, axis=0, keepdims=True)
    gains = jnp.concatenate([mixer_gain, feed_gain, jnp.zeros((14, WIDTH), F32)], axis=0)
    put(WEIGHT_ROWS, gains)
    if not want_grad_in:
        return None
    return (
        grad_middle.astype(F32) + norm_back(grad_scaled_a, normed_a, inverse_a, w.gain_mixer)
    ).astype(BF)


class Inputs:
    def __init__(self, names, sources, buffers, sems, block, early):
        self.block, self.copies = block, {}
        self.buffers = dict(zip(names, buffers, strict=True))
        for place, (name, source) in enumerate(zip(names, sources, strict=True)):
            self.copies[name] = pltpu.make_async_copy(source, self.buffers[name], sems.at[place])
        self.rest = list(self.copies.values())[early:]
        for copy in list(self.copies.values())[:early]:
            copy.start()

    def wait(self, *names):
        for name in names:
            if name in self.copies:
                self.copies.pop(name).wait()

    def start_rest(self):
        for copy in self.rest:
            copy.start()
        self.rest = []

    def __getattr__(self, name):
        if name not in self.__dict__.get("buffers", ()):
            raise AttributeError(name)
        self.wait(name)
        if name in GAINS:
            return self.buffers[name][self.block : self.block + 1, :]
        return self.buffers[name]


class Scratch:
    def __init__(self, names, refs, inputs=None):
        self.inputs = inputs
        for name, ref in zip(names, refs, strict=True):
            setattr(self, name, ref)

    def __getattr__(self, name):
        return getattr(self.__dict__["inputs"], name)

    def kept_weights(self, head):
        if self.inputs is None:
            return self.weights[head]
        piece, place = divmod(head, HEADS // PIECES)
        return getattr(self.inputs, f"weights{piece}")[place]


def as_column(row):
    wide = jnp.broadcast_to(row.astype(F32), (8, row.shape[1]))
    return wide.T[:, :1].astype(jnp.int32)


GAINS = ("gain_mixer", "gain_feed")
WEIGHTS = ("gain_mixer", "query", "key", "value", "out", "gain_feed", "up", "down")
FORWARD_SCRATCH = (
    ("query_t", (WIDTH, PATCH), BF),
    ("value_t", (WIDTH, PATCH), BF),
    ("bias", (PATCH, PATCH), F32),
    ("weights", (HEADS, PATCH, PATCH), BF),
    ("inverse_sum", (HEADS, 1, PATCH), F32),
    ("heads_t", (WIDTH, PATCH), BF),
)
BACKWARD_SCRATCH = (
    ("key_t", (WIDTH, PATCH), BF),
    ("grad_heads_t", (WIDTH, PATCH), BF),
    ("grad_query_t", (WIDTH, PATCH), BF),
    ("grad_key_t", (WIDTH, PATCH), BF),
    ("grad_value_t", (WIDTH, PATCH), BF),
    ("turned", (WIDTH, PATCH), BF),
    ("hidden", (PATCH, HIDDEN), BF),
)


SCRATCH = {name: (shape, dtype) for name, shape, dtype in FORWARD_SCRATCH + BACKWARD_SCRATCH}
VMEM_BYTES = 58 * 1024 * 1024


def project(scaled, w):
    query = dot(scaled, w.query[...]).astype(BF)
    key = dot(scaled, w.key[...]).astype(BF)
    value = dot(scaled, w.value[...]).astype(BF)
    return query, key, value


def forward(x, live_column, w, s, after_head=None):
    fill_bias(live_column, s.bias)
    normed, inverse, scaled = norm_rows(x, w.gain_mixer)
    query, key, value = project(scaled, w)
    w.start_rest()
    attend(query, key, value, s, after_head)
    heads_out = s.heads_t[...].astype(F32).T.astype(BF)
    middle = (x.astype(F32) + dot(heads_out, w.out[...])).astype(BF)
    return key, value, middle


def own_live(count):
    return (lax.broadcasted_iota(jnp.int32, (PATCH, 1), 0) < count).astype(jnp.int32)


def pack(rows, places, pairs_ref, packed_ref):
    slots = packed_ref.shape[0] // 2
    chosen = lax.broadcasted_iota(jnp.int32, (slots, PATCH), 0) == places[...]
    placed = dot(chosen.astype(BF), rows)
    pairs_ref[pl.ds(0, slots, 2), :] = placed[:, :LANES]
    pairs_ref[pl.ds(1, slots, 2), :] = placed[:, LANES:]
    packed_ref[...] = pairs_ref[...].astype(BF)


def unpack(arrived, places, pairs_ref):
    slots = arrived.shape[0] // 2
    pairs_ref[...] = arrived[...].astype(F32)
    placed = jnp.concatenate(
        [pairs_ref[pl.ds(0, slots, 2), :], pairs_ref[pl.ds(1, slots, 2), :]], axis=1
    ).astype(BF)
    columns = lax.broadcasted_iota(jnp.int32, (PATCH, slots), 1)
    return dot((columns == as_column(places[...])).astype(BF), placed).astype(BF)


def first_kernel(w, outs, scratch):
    packed_ref = outs[0]
    pairs_ref, sems, kept_sems = scratch[-3:]
    s = Scratch(
        ("value_t", "bias", "weights", "query_t", "heads_t", "inverse_sum", "key_rows",
         "value_rows", "middle_rows"),
        scratch[:-3],
    )
    started = []

    def keep(place, ref):
        copy = pltpu.make_async_copy(ref, outs[place], kept_sems.at[place - 1])
        copy.start()
        started.append(copy)

    def kept_copy(head):
        return pltpu.make_async_copy(s.weights.at[head], outs[7].at[head], sems.at[head])

    live = own_live(w.counts[lax.axis_index("patch")])
    x = w.rows[...].reshape(PATCH, WIDTH)
    key, value, middle = forward(x, live, w, s, lambda head: kept_copy(head).start())
    s.key_rows[...] = key
    s.value_rows[...] = value
    s.middle_rows[...] = middle
    for place, ref in enumerate(
        (s.key_rows, s.value_rows, s.middle_rows, s.query_t, s.heads_t, s.inverse_sum), 1
    ):
        keep(place, ref)
    _, _, _, pre = feed_forward(middle, w.up[...], w.gain_feed)
    block_out = (middle.astype(F32) + dot(gelu(pre).astype(BF), w.down[...])).astype(BF)
    pack(block_out, w.depart, pairs_ref, packed_ref)

    for head in range(HEADS):
        kept_copy(head).wait()
    for copy in started:
        copy.wait()


def second_kernel(w, outs, scratch):
    out_ref, keep_ref, give_ref, packed_ref = outs
    s = Scratch(SCRATCH, scratch[:-2])
    rows_ref, pairs_ref = scratch[-2:]
    part = lax.axis_index("mp")
    core = lax.rem(lax.axis_index("patch"), 2)
    x = unpack(w.arrived, w.arrive, pairs_ref)
    key, value, middle = forward(x, as_column(w.live[...]), w, s)
    own = pl.ds(pl.multiple_of(part * (PATCH // 4), PATCH // 4), PATCH // 4)
    rows_ref[...] = middle
    middle_part = rows_ref[own, :]
    _, _, _, pre = feed_forward(middle_part, w.up[...], w.gain_feed)
    out_ref[...] = (
        middle_part.astype(F32) + dot(gelu(pre).astype(BF), w.down[...])
    ).astype(BF)
    cotangent = w.cotangent[...].reshape(PATCH, WIDTH)
    grad_in = backward(
        part, core, cotangent, x, middle, key, value, w, s, (keep_ref, give_ref), True
    )
    pack(grad_in, w.arrive, pairs_ref, packed_ref)


def last_kernel(w, outs, scratch):
    s = Scratch([name for name, _, _ in BACKWARD_SCRATCH], scratch[:-3], w)
    halves, pairs_ref = scratch[-3:-1], scratch[-1]
    w.start_rest()
    grad_rows = unpack(w.arrived, w.depart, pairs_ref)
    middle = w.middle[...]
    backward(
        lax.axis_index("mp"), lax.rem(lax.axis_index("patch"), 2), grad_rows, w.rows, middle,
        w.key_rows, w.value_rows, w, s, halves, False,
    )
    chips = outs[0].shape[0]
    for out_ref, half, second in zip(outs, halves, (w.second_keep, w.second_give), strict=True):
        second = second[...].astype(F32)
        rows = jnp.concatenate([half[:WEIGHT_ROWS, :], second[:WEIGHT_ROWS, :]], axis=0)
        gains = jnp.concatenate(
            [
                half[WEIGHT_ROWS : WEIGHT_ROWS + 2, :],
                second[WEIGHT_ROWS : WEIGHT_ROWS + 2, :],
                jnp.zeros((4, LANES), F32),
            ],
            axis=0,
        )
        out_ref[...] = jnp.concatenate(
            [
                rows.reshape(chips, rows.shape[0] // chips, LANES),
                jnp.broadcast_to(gains[None], (chips, 8, LANES)),
            ],
            axis=1,
        ).astype(BF)


def finish_kernel(w, outs, scratch):
    mixer_ref, query_ref, key_ref, value_ref, out_ref, feed_ref, up_ref, down_ref = outs
    own_ref, other_ref = w.own, w.other
    core = lax.rem(lax.axis_index("patch"), 2)
    share = 2 * WEIGHT_ROWS // own_ref.shape[0]
    own_rows = own_ref[...].astype(F32)[:, :share, :].reshape(2 * WEIGHT_ROWS, LANES)
    other_rows = other_ref[...].astype(F32)[:, :share, :].reshape(2 * WEIGHT_ROWS, LANES)

    def join(own, other):
        low = jnp.where(core == 0, own, other)
        return jnp.concatenate([low, jnp.where(core == 0, other, own)], axis=1)

    gains = join(own_ref[0].astype(F32)[share:, :], other_ref[0].astype(F32)[share:, :])
    for block in range(2):

        def rows(first, size):
            there = slice(WEIGHT_ROWS * block + first, WEIGHT_ROWS * block + first + size)
            return join(own_rows[there, :], other_rows[there, :])

        for place, ref in enumerate((query_ref, key_ref, value_ref, out_ref)):
            ref[block] = rows(64 * place, 64)
        for piece in range(4):
            up_ref[block, :, WIDTH * piece : WIDTH * (piece + 1)] = rows(256 + 64 * piece, 64)
        down_ref[block] = rows(512, 256)
        mixer_ref[block : block + 1, :] = gains[2 * block : 2 * block + 1, :]
        feed_ref[block : block + 1, :] = gains[2 * block + 1 : 2 * block + 2, :]


def whole(array):
    zeros = (0,) * len(array.shape)
    return pl.BlockSpec(array.shape, lambda step: zeros)


HBM = pl.BlockSpec(memory_space=pltpu.HBM)


def part_shape(shape, part):
    kept = [
        (place.size,) if isinstance(place, pl.Slice) else () if isinstance(place, int) else (size,)
        for size, place in zip(shape, part or ())
    ]
    return sum(kept, ()) + shape[len(kept) :]


def call(kernel, inputs, weights, block, early, outputs, scratch, name):
    inputs = [(name, array, part) for name, array, part in inputs]
    inputs += [
        (weight, array, None if weight in GAINS else (block,))
        for weight, array in zip(WEIGHTS, weights)
    ]
    inputs.sort(key=lambda entry: early.index(entry[0]) if entry[0] in early else len(early))
    names = [name for name, _, _ in inputs]
    parts = [part for _, _, part in inputs]
    arrays = [array for _, array, _ in inputs]
    shapes = [
        jax.ShapeDtypeStruct(part_shape(array.shape, part), array.dtype)
        for array, part in zip(arrays, parts)
    ]
    buffers = [
        pltpu.SMEM(shape.shape, shape.dtype)
        if name == "counts"
        else pltpu.VMEM(shape.shape, shape.dtype)
        for name, shape in zip(names, shapes)
    ]
    first_out, first_scratch = len(arrays), len(arrays) + len(outputs)
    first_buffer = first_scratch + len(scratch)

    def whole_kernel(*refs):
        sources = [
            ref if part is None else ref.at[part] for ref, part in zip(refs[:first_out], parts)
        ]
        taken = Inputs(names, sources, refs[first_buffer:-1], refs[-1], block, len(early))
        kernel(taken, refs[first_out:first_scratch], refs[first_scratch:first_buffer])

    return pl.pallas_call(
        whole_kernel,
        grid=(1,),
        out_shape=[shape for shape, _ in outputs],
        in_specs=[HBM] * len(arrays),
        out_specs=[spec or whole(shape) for shape, spec in outputs],
        scratch_shapes=[*scratch, *buffers, pltpu.SemaphoreType.DMA((len(arrays),))],
        compiler_params=pltpu.CompilerParams(
            vmem_limit_bytes=VMEM_BYTES if weights else VMEM_BYTES // 4
        ),
        name=name,
    )(*arrays)


def vmem(*names):
    return [pltpu.VMEM(SCRATCH[name][0], SCRATCH[name][1]) for name in names]


def first_call(counts, gathered, depart, weights, buffer_rows):
    rows = jax.ShapeDtypeStruct((PATCH, WIDTH), BF)
    turned = jax.ShapeDtypeStruct((WIDTH, PATCH), BF)
    return call(
        first_kernel,
        [("rows", gathered, (slice(None), 0)), ("counts", counts, None), ("depart", depart, None)],
        weights,
        0,
        ("rows", "gain_mixer", "query", "key", "value", "counts"),
        [(jax.ShapeDtypeStruct((buffer_rows, LANES), BF), None)]
        + [(rows, HBM)] * 3
        + [(turned, HBM)] * 2
        + [
            (jax.ShapeDtypeStruct((HEADS, 1, PATCH), F32), HBM),
            (jax.ShapeDtypeStruct((HEADS, PATCH, PATCH), BF), HBM),
        ],
        vmem("value_t", "bias", "weights", "query_t", "heads_t", "inverse_sum")
        + [pltpu.VMEM((PATCH, WIDTH), BF)] * 3
        + [pltpu.VMEM((buffer_rows, LANES), F32)]
        + [pltpu.SemaphoreType.DMA((HEADS,)), pltpu.SemaphoreType.DMA((6,))],
        "first_block",
    )


def second_call(arrived, live, arrive, gathered, weights):
    half = jax.ShapeDtypeStruct((HALF_ROWS, LANES), BF)
    return call(
        second_kernel,
        [
            ("arrive", arrive, None), ("arrived", arrived, None), ("live", live, None),
            ("cotangent", gathered, (slice(None), 1)),
        ],
        weights,
        1,
        ("arrive", "arrived", "gain_mixer", "query", "key", "value", "live"),
        [
            (jax.ShapeDtypeStruct((PATCH // 4, WIDTH), BF), None), (half, None), (half, None),
            (jax.ShapeDtypeStruct(arrived.shape, BF), None),
        ],
        vmem(*SCRATCH) + [pltpu.VMEM((PATCH, WIDTH), BF), pltpu.VMEM(arrived.shape, F32)],
        "second_block",
    )


def last_call(arrived, depart, gathered, kept, second, weights, chips):
    key, value, middle, query_t, heads_t, inverse, attention = kept
    terms = jax.ShapeDtypeStruct((chips, 32, LANES), BF)
    return call(
        last_kernel,
        [
            ("depart", depart, None), ("arrived", arrived, None), ("middle", middle, None),
            ("heads_t", heads_t, None), ("rows", gathered, (slice(None), 0)),
            ("key_rows", key, None), ("value_rows", value, None), ("query_t", query_t, None),
            ("inverse_sum", inverse, None), ("second_keep", second[0], None),
            ("second_give", second[1], None),
        ]
        + [
            (f"weights{piece}", attention, (pl.ds(piece * HEADS // PIECES, HEADS // PIECES),))
            for piece in range(PIECES)
        ],
        weights,
        0,
        ("depart", "arrived", "middle", "gain_feed", "up", "down"),
        [(terms, None), (terms, None)],
        vmem(*[name for name, _, _ in BACKWARD_SCRATCH])
        + [pltpu.VMEM((HALF_ROWS, LANES), F32)] * 2
        + [pltpu.VMEM(arrived.shape, F32)],
        "first_block_back",
    )


def finish_call(own, other):
    gain = jax.ShapeDtypeStruct((2, WIDTH), F32)
    small = jax.ShapeDtypeStruct((2, WIDTH // 4, WIDTH), F32)
    up = jax.ShapeDtypeStruct((2, WIDTH // 4, HIDDEN), F32)
    down = jax.ShapeDtypeStruct((2, HIDDEN // 4, WIDTH), F32)
    return call(
        finish_kernel,
        [("own", own, None), ("other", other, None)],
        (),
        0,
        ("own", "other"),
        [(shape, None) for shape in (gain, small, small, small, small, gain, up, down)],
        [],
        "finish",
    )


def exchange_rows(buffer):
    peers = lax.axis_size("patch")
    shaped = buffer.reshape(peers, buffer.shape[0] // (2 * peers), 2, LANES)
    return exchange(shaped).reshape(buffer.shape)


def exchange(buffer, groups=None):
    return lax.all_to_all(
        buffer, "patch", split_axis=0, concat_axis=0, tiled=True, axis_index_groups=groups
    )


def swap_cores(half, peer_count):
    return lax.ppermute(half, "patch", [(i, i ^ 1) for i in range(peer_count)])


def body(
    points,
    patch_counts,
    to_hilbert,
    from_hilbert,
    cotangent,
    gain_mixer,
    query_weight,
    key_weight,
    value_weight,
    out_weight,
    gain_feed,
    up_weight,
    down_weight,
):
    peer_count = lax.axis_size("patch")
    buffer_rows = 2 * peer_count * SLOTS
    position = jnp.arange(PATCH, dtype=jnp.int32)

    def places(owners, ranking):
        ahead = (owners[:, None] == owners[None, :]) & (ranking[None, :] < ranking[:, None])
        return owners * SLOTS + jnp.sum(ahead.astype(jnp.int32), axis=1)

    depart = places(to_hilbert // PATCH, position)
    arrive = places(from_hilbert // PATCH, from_hilbert)
    source_patch = from_hilbert // PATCH
    source_count = jnp.sum(
        jnp.where(
            source_patch[:, None] == jnp.arange(peer_count, dtype=jnp.int32)[None, :],
            patch_counts[None, :],
            0,
        ),
        axis=1,
    )
    live_hilbert = (from_hilbert % PATCH < source_count).astype(jnp.int32)
    weights = (
        gain_mixer,
        query_weight,
        key_weight,
        value_weight,
        out_weight,
        gain_feed,
        up_weight,
        down_weight,
    )
    pair = jnp.stack([points, cotangent])
    pair = jnp.broadcast_to(pair[None], (lax.axis_size("mp"),) + pair.shape)
    gathered = lax.all_to_all(pair, "mp", split_axis=0, concat_axis=0, tiled=True)
    sent, *kept = first_call(patch_counts, gathered, depart[None, :], weights, buffer_rows)
    arrived = exchange_rows(sent)
    hilbert_out, second_keep, second_give, grad_sent = second_call(
        arrived, live_hilbert[None, :], arrive[None, :], gathered, weights
    )
    grad_arrived = exchange_rows(grad_sent)
    chips = peer_count // 2
    keep, give = last_call(
        grad_arrived, depart[None, :], gathered, kept,
        (second_keep, second_give), weights, chips,
    )
    taken = swap_cores(give, peer_count)
    terms = (keep.astype(F32) + taken.astype(F32)).astype(BF)
    groups = [[2 * chip + core for chip in range(chips)] for core in range(2)]
    sums = jnp.sum(exchange(terms, groups).astype(F32), axis=0).astype(BF)
    own = exchange(jnp.broadcast_to(sums[None], (chips,) + sums.shape), groups)
    other = swap_cores(own, peer_count)
    return (hilbert_out, *finish_call(own, other))


def solution(mesh):
    split = P(("patch", "mp"), None)
    in_specs = (split, P(), P("patch"), P("patch"), split) + (P(),) * 8
    own_rows = P(None, "mp", None)
    out_specs = (split, P(), own_rows, own_rows, own_rows, own_rows, P(), own_rows, own_rows)
    return jax.shard_map(body, mesh=mesh, in_specs=in_specs, out_specs=out_specs, check_vma=False)
```

```python
import functools

import jax
import jax.numpy as jnp
from jax import lax
from jax.experimental import pallas as pl
from jax.experimental.pallas import tpu as pltpu
from jax.sharding import PartitionSpec as P

HEADS = 16
PATCH = 512
HEAD_DIM = 16
WIDTH = 256
HIDDEN = 1024
SLOTS = 6
PIECES = 1
VALUE_SCALE = 1024.0
ALLOWED = -0.0078125
LANES = 128
WEIGHT_ROWS = 768
HALF_ROWS = WEIGHT_ROWS + 16
GAIN_ROWS = 4
CHUNK_ROWS = 24 + GAIN_ROWS

EPSILON = 1e-05
GELU_SCALE = 0.7978845608028654
GELU_CUBIC = 0.044715

BF = jnp.bfloat16
F32 = jnp.float32


def dot(left, right, left_dim=1, right_dim=0):
    return lax.dot_general(
        left, right, (((left_dim,), (right_dim,)), ((), ())), preferred_element_type=F32
    )


def norm_rows(values, gain_row):
    widened = values.astype(F32)
    centered = widened - jnp.mean(widened, axis=1, keepdims=True)
    inverse = lax.rsqrt(jnp.mean(centered * centered, axis=1, keepdims=True) + EPSILON)
    normed = centered * inverse
    return normed, inverse, (normed * gain_row).astype(BF)


def norm_back(grad_scaled, normed, inverse, gain_row):
    grad_normed = grad_scaled * gain_row
    centered = grad_normed - jnp.mean(grad_normed, axis=1, keepdims=True)
    return inverse * (centered - normed * jnp.mean(grad_normed * normed, axis=1, keepdims=True))


def gelu(pre):
    tangent = jnp.tanh(GELU_SCALE * (pre + GELU_CUBIC * (pre * pre * pre)))
    return 0.5 * pre * (1.0 + tangent)


def gelu_pair(pre):
    squared = pre * pre
    tangent = jnp.tanh(GELU_SCALE * (pre + GELU_CUBIC * (squared * pre)))
    half = 0.5 * (1.0 + tangent)
    slopes = half + 0.5 * pre * (1.0 - tangent * tangent) * (
        GELU_SCALE + GELU_SCALE * 3.0 * GELU_CUBIC * squared
    )
    return pre * half, slopes


def flip(values):
    return values.astype(F32).T.astype(BF)


def head_rows(head):
    return slice(head * HEAD_DIM, (head + 1) * HEAD_DIM)


def fill_bias(live_column, bias_ref):
    keys = lax.broadcasted_iota(jnp.int32, (PATCH, PATCH), 0)
    queries = lax.broadcasted_iota(jnp.int32, (PATCH, PATCH), 1)
    allowed = (live_column > 0) | (keys == queries)
    bias_ref[...] = jnp.where(allowed, ALLOWED, -1e30)


def attend(query, key, value, s, after_head=None):
    s.query_t[...] = (query.astype(F32) * HEAD_DIM ** (-0.5)).T.astype(BF)
    s.value_t[...] = (value.astype(F32) * (1.0 / VALUE_SCALE)).T.astype(BF)

    for head in range(HEADS):
        rows = head_rows(head)
        weights = jnp.exp(dot(key[:, rows], s.query_t[rows, :]) + s.bias[...])
        inverse = 1.0 / jnp.sum(weights, axis=0, keepdims=True)
        s.inverse_sum[head] = inverse
        lowered = weights.astype(BF)
        s.weights[head] = lowered
        if after_head is not None:
            after_head(head)
        mixed = dot(s.value_t[rows, :], lowered)
        s.heads_t[rows, :] = (mixed * (inverse * VALUE_SCALE)).astype(BF)


def attend_back(key, value, grad_heads, s):
    s.key_t[...] = flip(key)
    s.grad_heads_t[...] = flip(grad_heads)
    query_t, heads_t, inverse_sum = s.query_t, s.heads_t, s.inverse_sum

    for head in range(HEADS):
        rows = head_rows(head)
        query_rows = query_t[rows, :]
        grad_rows = s.grad_heads_t[rows, :]
        probability = s.kept_weights(head).astype(F32) * inverse_sum[head]
        grad_wide = grad_rows.astype(F32) * HEAD_DIM ** (-0.5)
        inner = jnp.sum(grad_wide * heads_t[rows, :].astype(F32), axis=0, keepdims=True)
        grad_prob = dot(value[:, rows], grad_wide.astype(BF))
        grad_score = (probability * (grad_prob - inner)).astype(BF)
        s.grad_value_t[rows, :] = dot(grad_rows, probability.astype(BF), 1, 1).astype(BF)
        s.grad_query_t[rows, :] = dot(s.key_t[rows, :], grad_score).astype(BF)
        s.grad_key_t[rows, :] = (
            dot(query_rows, grad_score, 1, 1) * HEAD_DIM**0.5
        ).astype(BF)


def feed_forward(middle, up_weight, gain_feed):
    normed_m, inverse_m, scaled_m = norm_rows(middle, gain_feed)
    return normed_m, inverse_m, scaled_m, dot(scaled_m, up_weight)


def backward(part, core, grad_rows, x, middle, key, value, w, s, halves, want_grad_in):
    def put(first_row, grad):
        rows = slice(first_row, first_row + grad.shape[0])
        low, high = grad[:, :LANES], grad[:, LANES:]
        halves[0][rows, :] = jnp.where(core == 0, low, high).astype(halves[0].dtype)
        halves[1][rows, :] = jnp.where(core == 0, high, low).astype(halves[1].dtype)

    normed_m, inverse_m, scaled_m, pre = feed_forward(middle, w.up[...], w.gain_feed)
    activated, slopes = gelu_pair(pre)
    s.hidden[...] = activated.astype(BF)
    s.turned[...] = flip(scaled_m)
    quarter = pl.ds(pl.multiple_of(part * (WIDTH // 4), WIDTH // 4), WIDTH // 4)
    hidden_part = s.hidden[:, pl.ds(pl.multiple_of(part * WIDTH, WIDTH), WIDTH)]
    put(512, dot(hidden_part, grad_rows, 0, 0))
    grad_pre = (dot(grad_rows, w.down[...], 1, 1) * slopes).astype(BF)
    up_grad = dot(s.turned[quarter, :], grad_pre)
    for piece in range(4):
        put(256 + 64 * piece, up_grad[:, WIDTH * piece : WIDTH * (piece + 1)])
    grad_scaled_m = dot(grad_pre, w.up[...], 1, 1)
    feed_gain = jnp.sum(grad_scaled_m * normed_m, axis=0, keepdims=True)
    grad_middle = (
        grad_rows.astype(F32)
        + norm_back(grad_scaled_m, normed_m, inverse_m, w.gain_feed)
    ).astype(BF)
    put(192, dot(s.heads_t[quarter, :], grad_middle))
    grad_heads = dot(grad_middle, w.out[...], 1, 1).astype(BF)
    attend_back(key[...], value[...], grad_heads, s)
    normed_a, inverse_a, scaled_a = norm_rows(x[...].reshape(PATCH, WIDTH), w.gain_mixer)
    s.turned[...] = flip(scaled_a)
    scaled_part = s.turned[quarter, :]
    put(0, dot(scaled_part, s.grad_query_t[...], 1, 1))
    put(64, dot(scaled_part, s.grad_key_t[...], 1, 1))
    put(128, dot(scaled_part, s.grad_value_t[...], 1, 1))
    grad_scaled_a = (
        dot(w.query[...], s.grad_query_t[...])
        + dot(w.key[...], s.grad_key_t[...])
        + dot(w.value[...], s.grad_value_t[...])
    ).T
    mixer_gain = jnp.sum(grad_scaled_a * normed_a, axis=0, keepdims=True)
    gains = jnp.concatenate([mixer_gain, feed_gain, jnp.zeros((14, WIDTH), F32)], axis=0)
    put(WEIGHT_ROWS, gains)
    if not want_grad_in:
        return None
    return (
        grad_middle.astype(F32) + norm_back(grad_scaled_a, normed_a, inverse_a, w.gain_mixer)
    ).astype(BF)


class Inputs:
    def __init__(self, names, sources, buffers, sems, block, early):
        self.block, self.copies = block, {}
        self.buffers = dict(zip(names, buffers, strict=True))
        for place, (name, source) in enumerate(zip(names, sources, strict=True)):
            self.copies[name] = pltpu.make_async_copy(source, self.buffers[name], sems.at[place])
        self.rest = list(self.copies.values())[early:]
        for copy in list(self.copies.values())[:early]:
            copy.start()

    def wait(self, *names):
        for name in names:
            if name in self.copies:
                self.copies.pop(name).wait()

    def start_rest(self):
        for copy in self.rest:
            copy.start()
        self.rest = []

    def __getattr__(self, name):
        if name not in self.__dict__.get("buffers", ()):
            raise AttributeError(name)
        self.wait(name)
        if name in GAINS:
            return self.buffers[name][self.block : self.block + 1, :]
        return self.buffers[name]


class Scratch:
    def __init__(self, names, refs, inputs=None):
        self.inputs = inputs
        for name, ref in zip(names, refs, strict=True):
            setattr(self, name, ref)

    def __getattr__(self, name):
        return getattr(self.__dict__["inputs"], name)

    def kept_weights(self, head):
        if self.inputs is None:
            return self.weights[head]
        piece, place = divmod(head, HEADS // PIECES)
        return getattr(self.inputs, f"weights{piece}")[place]


def as_column(row):
    wide = jnp.broadcast_to(row.astype(F32), (8, row.shape[1]))
    return wide.T[:, :1].astype(jnp.int32)


GAINS = ("gain_mixer", "gain_feed")
WEIGHTS = ("gain_mixer", "query", "key", "value", "out", "gain_feed", "up", "down")
FORWARD_SCRATCH = (
    ("query_t", (WIDTH, PATCH), BF),
    ("value_t", (WIDTH, PATCH), BF),
    ("bias", (PATCH, PATCH), F32),
    ("weights", (HEADS, PATCH, PATCH), BF),
    ("inverse_sum", (HEADS, 1, PATCH), F32),
    ("heads_t", (WIDTH, PATCH), BF),
)
BACKWARD_SCRATCH = (
    ("key_t", (WIDTH, PATCH), BF),
    ("grad_heads_t", (WIDTH, PATCH), BF),
    ("grad_query_t", (WIDTH, PATCH), BF),
    ("grad_key_t", (WIDTH, PATCH), BF),
    ("grad_value_t", (WIDTH, PATCH), BF),
    ("turned", (WIDTH, PATCH), BF),
    ("hidden", (PATCH, HIDDEN), BF),
)


SCRATCH = {name: (shape, dtype) for name, shape, dtype in FORWARD_SCRATCH + BACKWARD_SCRATCH}
VMEM_BYTES = 58 * 1024 * 1024


def project(scaled, w):
    query = dot(scaled, w.query[...]).astype(BF)
    key = dot(scaled, w.key[...]).astype(BF)
    value = dot(scaled, w.value[...]).astype(BF)
    return query, key, value


def forward(x, live_column, w, s, after_head=None):
    fill_bias(live_column, s.bias)
    normed, inverse, scaled = norm_rows(x, w.gain_mixer)
    query, key, value = project(scaled, w)
    w.start_rest()
    attend(query, key, value, s, after_head)
    heads_out = s.heads_t[...].astype(F32).T.astype(BF)
    middle = (x.astype(F32) + dot(heads_out, w.out[...])).astype(BF)
    return key, value, middle


def own_live(count):
    return (lax.broadcasted_iota(jnp.int32, (PATCH, 1), 0) < count).astype(jnp.int32)


def block_of(rows):
    return lax.shift_right_logical(rows, PATCH.bit_length() - 1)


def places_of(targets, ranking):
    owners = block_of(targets)
    same = block_of(as_column(targets)) == owners
    ahead = same & (as_column(ranking) < ranking)
    return owners * SLOTS + jnp.sum(ahead.astype(F32), axis=0, keepdims=True).astype(jnp.int32)


def moved_live(sources, counts):
    column = as_column(sources)
    patches = lax.broadcasted_iota(jnp.int32, (PATCH, counts.shape[1]), 1)
    chosen = jnp.where(patches == block_of(column), counts.astype(F32), 0.0)
    count = jnp.sum(chosen, axis=1, keepdims=True).astype(jnp.int32)
    return ((column & (PATCH - 1)) < count).astype(jnp.int32)


def pack(rows, places, pairs_ref, packed_ref):
    slots = packed_ref.shape[0] // 2
    chosen = lax.broadcasted_iota(jnp.int32, (slots, PATCH), 0) == places[...]
    placed = dot(chosen.astype(BF), rows)
    pairs_ref[pl.ds(0, slots, 2), :] = placed[:, :LANES]
    pairs_ref[pl.ds(1, slots, 2), :] = placed[:, LANES:]
    packed_ref[...] = pairs_ref[...].astype(BF)


def unpack(arrived, places, pairs_ref):
    slots = arrived.shape[0] // 2
    pairs_ref[...] = arrived[...].astype(F32)
    placed = jnp.concatenate(
        [pairs_ref[pl.ds(0, slots, 2), :], pairs_ref[pl.ds(1, slots, 2), :]], axis=1
    ).astype(BF)
    columns = lax.broadcasted_iota(jnp.int32, (PATCH, slots), 1)
    return dot((columns == as_column(places[...])).astype(BF), placed).astype(BF)


def first_kernel(w, outs, scratch):
    packed_ref = outs[0]
    pairs_ref, sems, kept_sems = scratch[-3:]
    s = Scratch(
        ("value_t", "bias", "weights", "query_t", "heads_t", "inverse_sum", "key_rows",
         "value_rows", "middle_rows", "depart"),
        scratch[:-3],
    )
    started = []

    def keep(place, ref):
        copy = pltpu.make_async_copy(ref, outs[place], kept_sems.at[place - 1])
        copy.start()
        started.append(copy)

    def kept_copy(head):
        return pltpu.make_async_copy(s.weights.at[head], outs[7].at[head], sems.at[head])

    live = own_live(w.counts[lax.axis_index("patch")])
    x = w.rows[...].reshape(PATCH, WIDTH)
    key, value, middle = forward(x, live, w, s, lambda head: kept_copy(head).start())
    s.key_rows[...] = key
    s.value_rows[...] = value
    s.middle_rows[...] = middle
    for place, ref in enumerate(
        (s.key_rows, s.value_rows, s.middle_rows, s.query_t, s.heads_t, s.inverse_sum), 1
    ):
        keep(place, ref)
    _, _, _, pre = feed_forward(middle, w.up[...], w.gain_feed)
    block_out = (middle.astype(F32) + dot(gelu(pre).astype(BF), w.down[...])).astype(BF)
    targets = w.to_hilbert[...]
    s.depart[...] = places_of(targets, lax.broadcasted_iota(jnp.int32, targets.shape, 1))
    keep(8, s.depart)
    pack(block_out, s.depart, pairs_ref, packed_ref)

    for head in range(HEADS):
        kept_copy(head).wait()
    for copy in started:
        copy.wait()


def second_kernel(w, outs, scratch):
    out_ref, keep_ref, give_ref, packed_ref = outs
    s = Scratch(SCRATCH, scratch[:-2])
    rows_ref, pairs_ref = scratch[-2:]
    part = lax.axis_index("mp")
    core = lax.rem(lax.axis_index("patch"), 2)
    sources = w.from_hilbert[...]
    arrive = places_of(sources, sources)
    live = moved_live(sources, w.counts_row[...])
    x = unpack(w.arrived, arrive, pairs_ref)
    key, value, middle = forward(x, live, w, s)
    own = pl.ds(pl.multiple_of(part * (PATCH // 4), PATCH // 4), PATCH // 4)
    rows_ref[...] = middle
    middle_part = rows_ref[own, :]
    _, _, _, pre = feed_forward(middle_part, w.up[...], w.gain_feed)
    out_ref[...] = (
        middle_part.astype(F32) + dot(gelu(pre).astype(BF), w.down[...])
    ).astype(BF)
    cotangent = w.cotangent[...].reshape(PATCH, WIDTH)
    grad_in = backward(
        part, core, cotangent, x, middle, key, value, w, s, (keep_ref, give_ref), True
    )
    pack(grad_in, arrive, pairs_ref, packed_ref)


def last_kernel(w, outs, scratch):
    s = Scratch([name for name, _, _ in BACKWARD_SCRATCH], scratch[:-4], w)
    halves, pairs_ref, chunks_ref = scratch[-4:-2], scratch[-2], scratch[-1]
    w.start_rest()
    grad_rows = unpack(w.arrived, w.depart, pairs_ref)
    middle = w.middle[...]
    backward(
        lax.axis_index("mp"), lax.rem(lax.axis_index("patch"), 2), grad_rows, w.rows, middle,
        w.key_rows, w.value_rows, w, s, halves, False,
    )
    for out_ref, half, second in zip(outs, halves, (w.second_keep, w.second_give), strict=True):
        second = second[...].astype(F32)
        gains = jnp.concatenate(
            [half[WEIGHT_ROWS : WEIGHT_ROWS + 2, :], second[WEIGHT_ROWS : WEIGHT_ROWS + 2, :]],
            axis=0,
        )
        chips = out_ref.shape[0] // CHUNK_ROWS
        share = CHUNK_ROWS - GAIN_ROWS
        for chip in range(chips):
            block, first = divmod(chip * share, WEIGHT_ROWS)
            source = second if block else half
            there = chip * CHUNK_ROWS
            chunks_ref[there : there + share, :] = source[first : first + share, :]
            chunks_ref[there + share : there + CHUNK_ROWS, :] = gains
        out_ref[...] = chunks_ref[...].astype(BF)


def finish_kernel(w, outs, scratch):
    mixer_ref, query_ref, key_ref, value_ref, out_ref, feed_ref, up_ref, down_ref = outs
    own_ref, other_ref = w.own, w.other
    core = lax.rem(lax.axis_index("patch"), 2)
    own_rows, other_rows = own_ref[...].astype(F32), other_ref[...].astype(F32)

    def join(own, other):
        low = jnp.where(core == 0, own, other)
        return jnp.concatenate([low, jnp.where(core == 0, other, own)], axis=1)

    last = slice(2 * WEIGHT_ROWS, 2 * WEIGHT_ROWS + GAIN_ROWS)
    gains = join(own_rows[last, :], other_rows[last, :])
    for block in range(2):

        def rows(first, size):
            there = slice(WEIGHT_ROWS * block + first, WEIGHT_ROWS * block + first + size)
            return join(own_rows[there, :], other_rows[there, :])

        for place, ref in enumerate((query_ref, key_ref, value_ref, out_ref)):
            ref[block] = rows(64 * place, 64)
        for piece in range(4):
            up_ref[block, :, WIDTH * piece : WIDTH * (piece + 1)] = rows(256 + 64 * piece, 64)
        down_ref[block] = rows(512, 256)
        mixer_ref[block : block + 1, :] = gains[2 * block : 2 * block + 1, :]
        feed_ref[block : block + 1, :] = gains[2 * block + 1 : 2 * block + 2, :]


def whole(array):
    zeros = (0,) * len(array.shape)
    return pl.BlockSpec(array.shape, lambda step: zeros)


HBM = pl.BlockSpec(memory_space=pltpu.HBM)


def part_shape(shape, part):
    kept = [
        (place.size,) if isinstance(place, pl.Slice) else () if isinstance(place, int) else (size,)
        for size, place in zip(shape, part or ())
    ]
    return sum(kept, ()) + shape[len(kept) :]


def call(kernel, inputs, weights, block, early, outputs, scratch, name):
    inputs = [(name, array, part) for name, array, part in inputs]
    inputs += [
        (weight, array, None if weight in GAINS else (block,))
        for weight, array in zip(WEIGHTS, weights)
    ]
    inputs.sort(key=lambda entry: early.index(entry[0]) if entry[0] in early else len(early))
    names = [name for name, _, _ in inputs]
    parts = [part for _, _, part in inputs]
    arrays = [array for _, array, _ in inputs]
    shapes = [
        jax.ShapeDtypeStruct(part_shape(array.shape, part), array.dtype)
        for array, part in zip(arrays, parts)
    ]
    buffers = [
        pltpu.SMEM(shape.shape, shape.dtype)
        if name == "counts"
        else pltpu.VMEM(shape.shape, shape.dtype)
        for name, shape in zip(names, shapes)
    ]
    first_out, first_scratch = len(arrays), len(arrays) + len(outputs)
    first_buffer = first_scratch + len(scratch)

    def whole_kernel(*refs):
        sources = [
            ref if part is None else ref.at[part] for ref, part in zip(refs[:first_out], parts)
        ]
        taken = Inputs(names, sources, refs[first_buffer:-1], refs[-1], block, len(early))
        kernel(taken, refs[first_out:first_scratch], refs[first_scratch:first_buffer])

    return pl.pallas_call(
        whole_kernel,
        grid=(1,),
        out_shape=[shape for shape, _ in outputs],
        in_specs=[HBM] * len(arrays),
        out_specs=[spec or whole(shape) for shape, spec in outputs],
        scratch_shapes=[*scratch, *buffers, pltpu.SemaphoreType.DMA((len(arrays),))],
        compiler_params=pltpu.CompilerParams(
            vmem_limit_bytes=VMEM_BYTES if weights else VMEM_BYTES // 4
        ),
        name=name,
    )(*arrays)


def vmem(*names):
    return [pltpu.VMEM(SCRATCH[name][0], SCRATCH[name][1]) for name in names]


def first_call(counts, gathered, to_hilbert, weights, buffer_rows):
    rows = jax.ShapeDtypeStruct((PATCH, WIDTH), BF)
    turned = jax.ShapeDtypeStruct((WIDTH, PATCH), BF)
    return call(
        first_kernel,
        [("rows", gathered, (slice(None), 0)), ("counts", counts, None), ("to_hilbert", to_hilbert, None)],
        weights,
        0,
        ("rows", "gain_mixer", "query", "key", "value", "counts"),
        [(jax.ShapeDtypeStruct((buffer_rows, LANES), BF), None)]
        + [(rows, HBM)] * 3
        + [(turned, HBM)] * 2
        + [
            (jax.ShapeDtypeStruct((HEADS, 1, PATCH), F32), HBM),
            (jax.ShapeDtypeStruct((HEADS, PATCH, PATCH), BF), HBM),
            (jax.ShapeDtypeStruct((1, PATCH), jnp.int32), HBM),
        ],
        vmem("value_t", "bias", "weights", "query_t", "heads_t", "inverse_sum")
        + [pltpu.VMEM((PATCH, WIDTH), BF)] * 3
        + [pltpu.VMEM((1, PATCH), jnp.int32)]
        + [pltpu.VMEM((buffer_rows, LANES), F32)]
        + [pltpu.SemaphoreType.DMA((HEADS,)), pltpu.SemaphoreType.DMA((8,))],
        "first_block",
    )


def second_call(arrived, from_hilbert, counts, gathered, weights):
    half = jax.ShapeDtypeStruct((HALF_ROWS, LANES), BF)
    return call(
        second_kernel,
        [
            ("from_hilbert", from_hilbert, None), ("counts_row", counts, None),
            ("arrived", arrived, None),
            ("cotangent", gathered, (slice(None), 1)),
        ],
        weights,
        1,
        ("from_hilbert", "counts_row", "arrived", "gain_mixer", "query", "key", "value"),
        [
            (jax.ShapeDtypeStruct((PATCH // 4, WIDTH), BF), None), (half, None), (half, None),
            (jax.ShapeDtypeStruct(arrived.shape, BF), None),
        ],
        vmem(*SCRATCH) + [pltpu.VMEM((PATCH, WIDTH), BF), pltpu.VMEM(arrived.shape, F32)],
        "second_block",
    )


def last_call(arrived, gathered, kept, second, weights, chips):
    key, value, middle, query_t, heads_t, inverse, attention, depart = kept
    terms = jax.ShapeDtypeStruct((chips * CHUNK_ROWS, LANES), BF)
    return call(
        last_kernel,
        [
            ("depart", depart, None), ("arrived", arrived, None), ("middle", middle, None),
            ("heads_t", heads_t, None), ("rows", gathered, (slice(None), 0)),
            ("key_rows", key, None), ("value_rows", value, None), ("query_t", query_t, None),
            ("inverse_sum", inverse, None), ("second_keep", second[0], None),
            ("second_give", second[1], None),
        ]
        + [
            (f"weights{piece}", attention, (pl.ds(piece * HEADS // PIECES, HEADS // PIECES),))
            for piece in range(PIECES)
        ],
        weights,
        0,
        ("depart", "arrived", "middle", "gain_feed", "up", "down"),
        [(terms, None), (terms, None)],
        vmem(*[name for name, _, _ in BACKWARD_SCRATCH])
        + [pltpu.VMEM((HALF_ROWS, LANES), F32)] * 2
        + [pltpu.VMEM(arrived.shape, F32), pltpu.VMEM(terms.shape, F32)],
        "first_block_back",
    )


def finish_call(own, other):
    gain = jax.ShapeDtypeStruct((2, WIDTH), F32)
    small = jax.ShapeDtypeStruct((2, WIDTH // 4, WIDTH), F32)
    up = jax.ShapeDtypeStruct((2, WIDTH // 4, HIDDEN), F32)
    down = jax.ShapeDtypeStruct((2, HIDDEN // 4, WIDTH), F32)
    return call(
        finish_kernel,
        [("own", own, None), ("other", other, None)],
        (),
        0,
        ("own", "other"),
        [(shape, None) for shape in (gain, small, small, small, small, gain, up, down)],
        [],
        "finish",
    )


def exchange_rows(buffer):
    peers = lax.axis_size("patch")
    shaped = buffer.reshape(peers, buffer.shape[0] // (2 * peers), 2, LANES)
    return exchange(shaped).reshape(buffer.shape)


def exchange(buffer, groups=None):
    return lax.all_to_all(
        buffer, "patch", split_axis=0, concat_axis=0, tiled=True, axis_index_groups=groups
    )


def swap_cores(half, peer_count):
    return lax.ppermute(half, "patch", [(i, i ^ 1) for i in range(peer_count)])


def body(
    points,
    patch_counts,
    to_hilbert,
    from_hilbert,
    cotangent,
    gain_mixer,
    query_weight,
    key_weight,
    value_weight,
    out_weight,
    gain_feed,
    up_weight,
    down_weight,
):
    peer_count = lax.axis_size("patch")
    buffer_rows = 2 * peer_count * SLOTS
    weights = (
        gain_mixer,
        query_weight,
        key_weight,
        value_weight,
        out_weight,
        gain_feed,
        up_weight,
        down_weight,
    )
    pair = jnp.stack([points, cotangent])
    pair = jnp.broadcast_to(pair[None], (lax.axis_size("mp"),) + pair.shape)
    gathered = lax.all_to_all(pair, "mp", split_axis=0, concat_axis=0, tiled=True)
    sent, *kept = first_call(
        patch_counts, gathered, to_hilbert[None, :], weights, buffer_rows
    )
    arrived = exchange_rows(sent)
    hilbert_out, second_keep, second_give, grad_sent = second_call(
        arrived, from_hilbert[None, :], patch_counts[None, :], gathered, weights
    )
    grad_arrived = exchange_rows(grad_sent)
    chips = peer_count // 2
    keep, give = last_call(
        grad_arrived, gathered, kept, (second_keep, second_give), weights, chips,
    )
    taken = swap_cores(give, peer_count)
    terms = (keep.astype(F32) + taken.astype(F32)).astype(BF)
    groups = [[2 * chip + core for chip in range(chips)] for core in range(2)]
    arrived_terms = exchange(terms.reshape(chips, CHUNK_ROWS // 4, 4, LANES), groups)
    sums = jnp.sum(arrived_terms.astype(F32), axis=0).astype(BF).reshape(CHUNK_ROWS, LANES)
    share = CHUNK_ROWS - GAIN_ROWS
    spread = jnp.broadcast_to(sums[None, :share], (chips, share, LANES))
    own, sums = lax.optimization_barrier((exchange(spread, groups), sums))
    own = own.reshape(chips * share, LANES)
    own = jnp.concatenate([own, sums[share:], jnp.zeros((16 - GAIN_ROWS, LANES), BF)], axis=0)
    other = swap_cores(own, peer_count)
    return (hilbert_out, *finish_call(own, other))


def solution(mesh):
    split = P(("patch", "mp"), None)
    in_specs = (split, P(), P("patch"), P("patch"), split) + (P(),) * 8
    own_rows = P(None, "mp", None)
    out_specs = (split, P(), own_rows, own_rows, own_rows, own_rows, P(), own_rows, own_rows)
    return jax.shard_map(body, mesh=mesh, in_specs=in_specs, out_specs=out_specs, check_vma=False)
```

```python
import functools

import jax
import jax.numpy as jnp
from jax import lax
from jax.experimental import pallas as pl
from jax.experimental.pallas import tpu as pltpu
from jax.sharding import PartitionSpec as P

HEADS = 16
PATCH = 512
HEAD_DIM = 16
WIDTH = 256
HIDDEN = 1024
SLOTS = 6
PIECES = 1
VALUE_SCALE = 1024.0
ALLOWED = -0.0078125
LANES = 128
WEIGHT_ROWS = 768
HALF_ROWS = WEIGHT_ROWS + 16
GAIN_ROWS = 4
CHUNK_ROWS = 24 + GAIN_ROWS

EPSILON = 1e-05
GELU_SCALE = 0.7978845608028654
GELU_CUBIC = 0.044715

BF = jnp.bfloat16
F32 = jnp.float32


def dot(left, right, left_dim=1, right_dim=0):
    return lax.dot_general(
        left, right, (((left_dim,), (right_dim,)), ((), ())), preferred_element_type=F32
    )


def norm_rows(values, gain_row):
    widened = values.astype(F32)
    centered = widened - jnp.mean(widened, axis=1, keepdims=True)
    inverse = lax.rsqrt(jnp.mean(centered * centered, axis=1, keepdims=True) + EPSILON)
    normed = centered * inverse
    return normed, inverse, (normed * gain_row).astype(BF)


def norm_back(grad_scaled, normed, inverse, gain_row):
    grad_normed = grad_scaled * gain_row
    centered = grad_normed - jnp.mean(grad_normed, axis=1, keepdims=True)
    return inverse * (centered - normed * jnp.mean(grad_normed * normed, axis=1, keepdims=True))


def gelu(pre):
    tangent = jnp.tanh(GELU_SCALE * (pre + GELU_CUBIC * (pre * pre * pre)))
    return 0.5 * pre * (1.0 + tangent)


def gelu_pair(pre):
    squared = pre * pre
    tangent = jnp.tanh(GELU_SCALE * (pre + GELU_CUBIC * (squared * pre)))
    half = 0.5 * (1.0 + tangent)
    slopes = half + 0.5 * pre * (1.0 - tangent * tangent) * (
        GELU_SCALE + GELU_SCALE * 3.0 * GELU_CUBIC * squared
    )
    return pre * half, slopes


def flip(values):
    return values.astype(F32).T.astype(BF)


def head_rows(head):
    return slice(head * HEAD_DIM, (head + 1) * HEAD_DIM)


def fill_bias(live_column, bias_ref):
    keys = lax.broadcasted_iota(jnp.int32, (PATCH, PATCH), 0)
    queries = lax.broadcasted_iota(jnp.int32, (PATCH, PATCH), 1)
    allowed = (live_column > 0) | (keys == queries)
    bias_ref[...] = jnp.where(allowed, ALLOWED, -1e30)


def attend(query, key, value, s, after_head=None):
    s.query_t[...] = (query.astype(F32) * HEAD_DIM ** (-0.5)).T.astype(BF)
    s.value_t[...] = (value.astype(F32) * (1.0 / VALUE_SCALE)).T.astype(BF)

    for head in range(HEADS):
        rows = head_rows(head)
        weights = jnp.exp(dot(key[:, rows], s.query_t[rows, :]) + s.bias[...])
        inverse = 1.0 / jnp.sum(weights, axis=0, keepdims=True)
        s.inverse_sum[head] = inverse
        lowered = weights.astype(BF)
        s.weights[head] = lowered
        if after_head is not None:
            after_head(head)
        mixed = dot(s.value_t[rows, :], lowered)
        s.heads_t[rows, :] = (mixed * (inverse * VALUE_SCALE)).astype(BF)


def attend_back(key, value, grad_heads, s):
    s.key_t[...] = flip(key)
    s.grad_heads_t[...] = flip(grad_heads)
    query_t, heads_t, inverse_sum = s.query_t, s.heads_t, s.inverse_sum

    for head in range(HEADS):
        rows = head_rows(head)
        query_rows = query_t[rows, :]
        grad_rows = s.grad_heads_t[rows, :]
        probability = s.kept_weights(head).astype(F32) * inverse_sum[head]
        grad_wide = grad_rows.astype(F32) * HEAD_DIM ** (-0.5)
        inner = jnp.sum(grad_wide * heads_t[rows, :].astype(F32), axis=0, keepdims=True)
        grad_prob = dot(value[:, rows], grad_wide.astype(BF))
        grad_score = (probability * (grad_prob - inner)).astype(BF)
        s.grad_value_t[rows, :] = dot(grad_rows, probability.astype(BF), 1, 1).astype(BF)
        s.grad_query_t[rows, :] = dot(s.key_t[rows, :], grad_score).astype(BF)
        s.grad_key_t[rows, :] = (
            dot(query_rows, grad_score, 1, 1) * HEAD_DIM**0.5
        ).astype(BF)


def feed_forward(middle, up_weight, gain_feed):
    normed_m, inverse_m, scaled_m = norm_rows(middle, gain_feed)
    return normed_m, inverse_m, scaled_m, dot(scaled_m, up_weight)


def backward(part, core, grad_rows, x, middle, key, value, w, s, halves, want_grad_in):
    def put(first_row, grad):
        rows = slice(first_row, first_row + grad.shape[0])
        low, high = grad[:, :LANES], grad[:, LANES:]
        halves[0][rows, :] = jnp.where(core == 0, low, high).astype(halves[0].dtype)
        halves[1][rows, :] = jnp.where(core == 0, high, low).astype(halves[1].dtype)

    normed_m, inverse_m, scaled_m, pre = feed_forward(middle, w.up[...], w.gain_feed)
    activated, slopes = gelu_pair(pre)
    s.hidden[...] = activated.astype(BF)
    s.turned[...] = flip(scaled_m)
    quarter = pl.ds(pl.multiple_of(part * (WIDTH // 4), WIDTH // 4), WIDTH // 4)
    hidden_part = s.hidden[:, pl.ds(pl.multiple_of(part * WIDTH, WIDTH), WIDTH)]
    put(512, dot(hidden_part, grad_rows, 0, 0))
    grad_pre = (dot(grad_rows, w.down[...], 1, 1) * slopes).astype(BF)
    up_grad = dot(s.turned[quarter, :], grad_pre)
    for piece in range(4):
        put(256 + 64 * piece, up_grad[:, WIDTH * piece : WIDTH * (piece + 1)])
    grad_scaled_m = dot(grad_pre, w.up[...], 1, 1)
    feed_gain = jnp.sum(grad_scaled_m * normed_m, axis=0, keepdims=True)
    grad_middle = (
        grad_rows.astype(F32)
        + norm_back(grad_scaled_m, normed_m, inverse_m, w.gain_feed)
    ).astype(BF)
    put(192, dot(s.heads_t[quarter, :], grad_middle))
    grad_heads = dot(grad_middle, w.out[...], 1, 1).astype(BF)
    attend_back(key[...], value[...], grad_heads, s)
    normed_a, inverse_a, scaled_a = norm_rows(x[...].reshape(PATCH, WIDTH), w.gain_mixer)
    s.turned[...] = flip(scaled_a)
    scaled_part = s.turned[quarter, :]
    put(0, dot(scaled_part, s.grad_query_t[...], 1, 1))
    put(64, dot(scaled_part, s.grad_key_t[...], 1, 1))
    put(128, dot(scaled_part, s.grad_value_t[...], 1, 1))
    grad_scaled_a = (
        dot(w.query[...], s.grad_query_t[...])
        + dot(w.key[...], s.grad_key_t[...])
        + dot(w.value[...], s.grad_value_t[...])
    ).T
    mixer_gain = jnp.sum(grad_scaled_a * normed_a, axis=0, keepdims=True)
    gains = jnp.concatenate([mixer_gain, feed_gain, jnp.zeros((14, WIDTH), F32)], axis=0)
    put(WEIGHT_ROWS, gains)
    if not want_grad_in:
        return None
    return (
        grad_middle.astype(F32) + norm_back(grad_scaled_a, normed_a, inverse_a, w.gain_mixer)
    ).astype(BF)


class Inputs:
    def __init__(self, names, sources, buffers, sems, block, early):
        self.block, self.copies = block, {}
        self.buffers = dict(zip(names, buffers, strict=True))
        for place, (name, source) in enumerate(zip(names, sources, strict=True)):
            self.copies[name] = pltpu.make_async_copy(source, self.buffers[name], sems.at[place])
        self.rest = list(self.copies.values())[early:]
        for copy in list(self.copies.values())[:early]:
            copy.start()

    def wait(self, *names):
        for name in names:
            if name in self.copies:
                self.copies.pop(name).wait()

    def start_rest(self):
        for copy in self.rest:
            copy.start()
        self.rest = []

    def __getattr__(self, name):
        if name not in self.__dict__.get("buffers", ()):
            raise AttributeError(name)
        self.wait(name)
        if name in GAINS:
            return self.buffers[name][self.block : self.block + 1, :]
        return self.buffers[name]


class Scratch:
    def __init__(self, names, refs, inputs=None):
        self.inputs = inputs
        for name, ref in zip(names, refs, strict=True):
            setattr(self, name, ref)

    def __getattr__(self, name):
        return getattr(self.__dict__["inputs"], name)

    def kept_weights(self, head):
        if self.inputs is None:
            return self.weights[head]
        piece, place = divmod(head, HEADS // PIECES)
        return getattr(self.inputs, f"weights{piece}")[place]


def as_column(row):
    wide = jnp.broadcast_to(row.astype(F32), (8, row.shape[1]))
    return wide.T[:, :1].astype(jnp.int32)


GAINS = ("gain_mixer", "gain_feed")
WEIGHTS = ("gain_mixer", "query", "key", "value", "out", "gain_feed", "up", "down")
FORWARD_SCRATCH = (
    ("query_t", (WIDTH, PATCH), BF),
    ("value_t", (WIDTH, PATCH), BF),
    ("bias", (PATCH, PATCH), F32),
    ("weights", (HEADS, PATCH, PATCH), BF),
    ("inverse_sum", (HEADS, 1, PATCH), F32),
    ("heads_t", (WIDTH, PATCH), BF),
)
BACKWARD_SCRATCH = (
    ("key_t", (WIDTH, PATCH), BF),
    ("grad_heads_t", (WIDTH, PATCH), BF),
    ("grad_query_t", (WIDTH, PATCH), BF),
    ("grad_key_t", (WIDTH, PATCH), BF),
    ("grad_value_t", (WIDTH, PATCH), BF),
    ("turned", (WIDTH, PATCH), BF),
    ("hidden", (PATCH, HIDDEN), BF),
)


SCRATCH = {name: (shape, dtype) for name, shape, dtype in FORWARD_SCRATCH + BACKWARD_SCRATCH}
VMEM_BYTES = 58 * 1024 * 1024


def project(scaled, w):
    query = dot(scaled, w.query[...]).astype(BF)
    key = dot(scaled, w.key[...]).astype(BF)
    value = dot(scaled, w.value[...]).astype(BF)
    return query, key, value


def forward(x, live_column, w, s, after_head=None):
    fill_bias(live_column, s.bias)
    normed, inverse, scaled = norm_rows(x, w.gain_mixer)
    query, key, value = project(scaled, w)
    w.start_rest()
    attend(query, key, value, s, after_head)
    heads_out = s.heads_t[...].astype(F32).T.astype(BF)
    middle = (x.astype(F32) + dot(heads_out, w.out[...])).astype(BF)
    return key, value, middle


def own_live(count):
    return (lax.broadcasted_iota(jnp.int32, (PATCH, 1), 0) < count).astype(jnp.int32)


def block_of(rows):
    return lax.shift_right_logical(rows, PATCH.bit_length() - 1)


def places_of(targets, ranking):
    owners = block_of(targets)
    same = block_of(as_column(targets)) == owners
    ahead = same & (as_column(ranking) < ranking)
    return owners * SLOTS + jnp.sum(ahead.astype(F32), axis=0, keepdims=True).astype(jnp.int32)


def moved_live(sources, counts):
    column = as_column(sources)
    patches = lax.broadcasted_iota(jnp.int32, (PATCH, counts.shape[1]), 1)
    chosen = jnp.where(patches == block_of(column), counts.astype(F32), 0.0)
    count = jnp.sum(chosen, axis=1, keepdims=True).astype(jnp.int32)
    return ((column & (PATCH - 1)) < count).astype(jnp.int32)


def pack(rows, places, pairs_ref, packed_ref):
    slots = packed_ref.shape[0] // 2
    chosen = lax.broadcasted_iota(jnp.int32, (slots, PATCH), 0) == places[...]
    placed = dot(chosen.astype(BF), rows)
    pairs_ref[pl.ds(0, slots, 2), :] = placed[:, :LANES]
    pairs_ref[pl.ds(1, slots, 2), :] = placed[:, LANES:]
    packed_ref[...] = pairs_ref[...].astype(BF)


def unpack(arrived, places, pairs_ref):
    slots = arrived.shape[0] // 2
    pairs_ref[...] = arrived[...].astype(F32)
    placed = jnp.concatenate(
        [pairs_ref[pl.ds(0, slots, 2), :], pairs_ref[pl.ds(1, slots, 2), :]], axis=1
    ).astype(BF)
    columns = lax.broadcasted_iota(jnp.int32, (PATCH, slots), 1)
    return dot((columns == as_column(places[...])).astype(BF), placed).astype(BF)


def first_kernel(w, outs, scratch):
    packed_ref = outs[0]
    pairs_ref, sems, kept_sems = scratch[-3:]
    s = Scratch(
        ("value_t", "bias", "weights", "query_t", "heads_t", "inverse_sum", "key_rows",
         "value_rows", "middle_rows", "depart"),
        scratch[:-3],
    )
    started = []

    def keep(place, ref):
        copy = pltpu.make_async_copy(ref, outs[place], kept_sems.at[place - 1])
        copy.start()
        started.append(copy)

    def kept_copy(head):
        return pltpu.make_async_copy(s.weights.at[head], outs[7].at[head], sems.at[head])

    live = own_live(w.counts[lax.axis_index("patch")])
    x = w.rows[...].reshape(PATCH, WIDTH)
    key, value, middle = forward(x, live, w, s, lambda head: kept_copy(head).start())
    s.key_rows[...] = key
    s.value_rows[...] = value
    s.middle_rows[...] = middle
    for place, ref in enumerate(
        (s.key_rows, s.value_rows, s.middle_rows, s.query_t, s.heads_t, s.inverse_sum), 1
    ):
        keep(place, ref)
    _, _, _, pre = feed_forward(middle, w.up[...], w.gain_feed)
    block_out = (middle.astype(F32) + dot(gelu(pre).astype(BF), w.down[...])).astype(BF)
    targets = w.to_hilbert[...]
    s.depart[...] = places_of(targets, lax.broadcasted_iota(jnp.int32, targets.shape, 1))
    keep(8, s.depart)
    pack(block_out, s.depart, pairs_ref, packed_ref)

    for head in range(HEADS):
        kept_copy(head).wait()
    for copy in started:
        copy.wait()


def second_kernel(w, outs, scratch):
    out_ref, keep_ref, give_ref, packed_ref = outs
    s = Scratch(SCRATCH, scratch[:-2])
    rows_ref, pairs_ref = scratch[-2:]
    part = lax.axis_index("mp")
    core = lax.rem(lax.axis_index("patch"), 2)
    sources = w.from_hilbert[...]
    arrive = places_of(sources, sources)
    live = moved_live(sources, w.counts_row[...])
    x = unpack(w.arrived, arrive, pairs_ref)
    key, value, middle = forward(x, live, w, s)
    own = pl.ds(pl.multiple_of(part * (PATCH // 4), PATCH // 4), PATCH // 4)
    rows_ref[...] = middle
    middle_part = rows_ref[own, :]
    _, _, _, pre = feed_forward(middle_part, w.up[...], w.gain_feed)
    out_ref[...] = (
        middle_part.astype(F32) + dot(gelu(pre).astype(BF), w.down[...])
    ).astype(BF)
    cotangent = w.cotangent[...].reshape(PATCH, WIDTH)
    grad_in = backward(
        part, core, cotangent, x, middle, key, value, w, s, (keep_ref, give_ref), True
    )
    pack(grad_in, arrive, pairs_ref, packed_ref)


def last_kernel(w, outs, scratch):
    s = Scratch([name for name, _, _ in BACKWARD_SCRATCH], scratch[:-4], w)
    halves, pairs_ref, chunks_ref = scratch[-4:-2], scratch[-2], scratch[-1]
    w.start_rest()
    grad_rows = unpack(w.arrived, w.depart, pairs_ref)
    middle = w.middle[...]
    backward(
        lax.axis_index("mp"), lax.rem(lax.axis_index("patch"), 2), grad_rows, w.rows, middle,
        w.key_rows, w.value_rows, w, s, halves, False,
    )
    for out_ref, half, second in zip(outs, halves, (w.second_keep, w.second_give), strict=True):
        second = second[...].astype(F32)
        gains = jnp.concatenate(
            [half[WEIGHT_ROWS : WEIGHT_ROWS + 2, :], second[WEIGHT_ROWS : WEIGHT_ROWS + 2, :]],
            axis=0,
        )
        chips = out_ref.shape[0] // CHUNK_ROWS
        share = CHUNK_ROWS - GAIN_ROWS
        for chip in range(chips):
            block, first = divmod(chip * share, WEIGHT_ROWS)
            source = second if block else half
            there = chip * CHUNK_ROWS
            chunks_ref[there : there + share, :] = source[first : first + share, :]
            chunks_ref[there + share : there + CHUNK_ROWS, :] = gains
        out_ref[...] = chunks_ref[...].astype(BF)


def finish_kernel(w, outs, scratch):
    mixer_ref, query_ref, key_ref, value_ref, out_ref, feed_ref, up_ref, down_ref = outs
    own_ref, other_ref = w.own, w.other
    core = lax.rem(lax.axis_index("patch"), 2)
    own_rows, other_rows = own_ref[...].astype(F32), other_ref[...].astype(F32)

    def join(own, other):
        low = jnp.where(core == 0, own, other)
        return jnp.concatenate([low, jnp.where(core == 0, other, own)], axis=1)

    last = slice(2 * WEIGHT_ROWS, 2 * WEIGHT_ROWS + GAIN_ROWS)
    gains = join(own_rows[last, :], other_rows[last, :])
    for block in range(2):

        def rows(first, size):
            there = slice(WEIGHT_ROWS * block + first, WEIGHT_ROWS * block + first + size)
            return join(own_rows[there, :], other_rows[there, :])

        for place, ref in enumerate((query_ref, key_ref, value_ref, out_ref)):
            ref[block] = rows(64 * place, 64)
        for piece in range(4):
            up_ref[block, :, WIDTH * piece : WIDTH * (piece + 1)] = rows(256 + 64 * piece, 64)
        down_ref[block] = rows(512, 256)
        mixer_ref[block : block + 1, :] = gains[2 * block : 2 * block + 1, :]
        feed_ref[block : block + 1, :] = gains[2 * block + 1 : 2 * block + 2, :]


def whole(array):
    zeros = (0,) * len(array.shape)
    return pl.BlockSpec(array.shape, lambda step: zeros)


HBM = pl.BlockSpec(memory_space=pltpu.HBM)


def part_shape(shape, part):
    kept = [
        (place.size,) if isinstance(place, pl.Slice) else () if isinstance(place, int) else (size,)
        for size, place in zip(shape, part or ())
    ]
    return sum(kept, ()) + shape[len(kept) :]


def call(
    kernel, inputs, weights, block, early, outputs, scratch, name, vmem_bytes=VMEM_BYTES
):
    inputs = [(name, array, part) for name, array, part in inputs]
    inputs += [
        (weight, array, None if weight in GAINS else (block,))
        for weight, array in zip(WEIGHTS, weights)
    ]
    inputs.sort(key=lambda entry: early.index(entry[0]) if entry[0] in early else len(early))
    names = [name for name, _, _ in inputs]
    parts = [part for _, _, part in inputs]
    arrays = [array for _, array, _ in inputs]
    shapes = [
        jax.ShapeDtypeStruct(part_shape(array.shape, part), array.dtype)
        for array, part in zip(arrays, parts)
    ]
    buffers = [
        pltpu.SMEM(shape.shape, shape.dtype)
        if name == "counts"
        else pltpu.VMEM(shape.shape, shape.dtype)
        for name, shape in zip(names, shapes)
    ]
    first_out, first_scratch = len(arrays), len(arrays) + len(outputs)
    first_buffer = first_scratch + len(scratch)

    def whole_kernel(*refs):
        sources = [
            ref if part is None else ref.at[part] for ref, part in zip(refs[:first_out], parts)
        ]
        taken = Inputs(names, sources, refs[first_buffer:-1], refs[-1], block, len(early))
        kernel(taken, refs[first_out:first_scratch], refs[first_scratch:first_buffer])

    return pl.pallas_call(
        whole_kernel,
        grid=(1,),
        out_shape=[shape for shape, _ in outputs],
        in_specs=[HBM] * len(arrays),
        out_specs=[spec or whole(shape) for shape, spec in outputs],
        scratch_shapes=[*scratch, *buffers, pltpu.SemaphoreType.DMA((len(arrays),))],
        compiler_params=pltpu.CompilerParams(
            vmem_limit_bytes=vmem_bytes
        ),
        name=name,
    )(*arrays)


def vmem(*names):
    return [pltpu.VMEM(SCRATCH[name][0], SCRATCH[name][1]) for name in names]


def first_call(counts, gathered, to_hilbert, weights, buffer_rows):
    rows = jax.ShapeDtypeStruct((PATCH, WIDTH), BF)
    turned = jax.ShapeDtypeStruct((WIDTH, PATCH), BF)
    return call(
        first_kernel,
        [("rows", gathered, (slice(None), 0)), ("counts", counts, None), ("to_hilbert", to_hilbert, None)],
        weights,
        0,
        ("rows", "gain_mixer", "query", "key", "value", "counts"),
        [(jax.ShapeDtypeStruct((buffer_rows, LANES), BF), None)]
        + [(rows, HBM)] * 3
        + [(turned, HBM)] * 2
        + [
            (jax.ShapeDtypeStruct((HEADS, 1, PATCH), F32), HBM),
            (jax.ShapeDtypeStruct((HEADS, PATCH, PATCH), BF), HBM),
            (jax.ShapeDtypeStruct((1, PATCH), jnp.int32), HBM),
        ],
        vmem("value_t", "bias", "weights", "query_t", "heads_t", "inverse_sum")
        + [pltpu.VMEM((PATCH, WIDTH), BF)] * 3
        + [pltpu.VMEM((1, PATCH), jnp.int32)]
        + [pltpu.VMEM((buffer_rows, LANES), F32)]
        + [pltpu.SemaphoreType.DMA((HEADS,)), pltpu.SemaphoreType.DMA((8,))],
        "first_block",
    )


def second_call(arrived, from_hilbert, counts, gathered, weights):
    half = jax.ShapeDtypeStruct((HALF_ROWS, LANES), BF)
    return call(
        second_kernel,
        [
            ("from_hilbert", from_hilbert, None), ("counts_row", counts, None),
            ("arrived", arrived, None),
            ("cotangent", gathered, (slice(None), 1)),
        ],
        weights,
        1,
        ("from_hilbert", "counts_row", "arrived", "gain_mixer", "query", "key", "value"),
        [
            (jax.ShapeDtypeStruct((PATCH // 4, WIDTH), BF), None), (half, None), (half, None),
            (jax.ShapeDtypeStruct(arrived.shape, BF), None),
        ],
        vmem(*SCRATCH) + [pltpu.VMEM((PATCH, WIDTH), BF), pltpu.VMEM(arrived.shape, F32)],
        "second_block",
    )


def last_call(arrived, gathered, kept, second, weights, chips):
    key, value, middle, query_t, heads_t, inverse, attention, depart = kept
    terms = jax.ShapeDtypeStruct((chips * CHUNK_ROWS, LANES), BF)
    return call(
        last_kernel,
        [
            ("depart", depart, None), ("arrived", arrived, None), ("middle", middle, None),
            ("heads_t", heads_t, None), ("rows", gathered, (slice(None), 0)),
            ("key_rows", key, None), ("value_rows", value, None), ("query_t", query_t, None),
            ("inverse_sum", inverse, None), ("second_keep", second[0], None),
            ("second_give", second[1], None),
        ]
        + [
            (f"weights{piece}", attention, (pl.ds(piece * HEADS // PIECES, HEADS // PIECES),))
            for piece in range(PIECES)
        ],
        weights,
        0,
        ("depart", "arrived", "middle", "gain_feed", "up", "down"),
        [(terms, None), (terms, None)],
        vmem(*[name for name, _, _ in BACKWARD_SCRATCH])
        + [pltpu.VMEM((HALF_ROWS, LANES), F32)] * 2
        + [pltpu.VMEM(arrived.shape, F32), pltpu.VMEM(terms.shape, F32)],
        "first_block_back",
        40 * 1024 * 1024,
    )


def finish_call(own, other):
    gain = jax.ShapeDtypeStruct((2, WIDTH), F32)
    small = jax.ShapeDtypeStruct((2, WIDTH // 4, WIDTH), F32)
    up = jax.ShapeDtypeStruct((2, WIDTH // 4, HIDDEN), F32)
    down = jax.ShapeDtypeStruct((2, HIDDEN // 4, WIDTH), F32)
    return call(
        finish_kernel,
        [("own", own, None), ("other", other, None)],
        (),
        0,
        ("own", "other"),
        [(shape, None) for shape in (gain, small, small, small, small, gain, up, down)],
        [],
        "finish",
        VMEM_BYTES // 4,
    )


def exchange_rows(buffer):
    peers = lax.axis_size("patch")
    shaped = buffer.reshape(peers, buffer.shape[0] // (2 * peers), 2, LANES)
    return exchange(shaped).reshape(buffer.shape)


def exchange(buffer, groups=None):
    return lax.all_to_all(
        buffer, "patch", split_axis=0, concat_axis=0, tiled=True, axis_index_groups=groups
    )


def swap_cores(half, peer_count):
    return lax.ppermute(half, "patch", [(i, i ^ 1) for i in range(peer_count)])


def body(
    points,
    patch_counts,
    to_hilbert,
    from_hilbert,
    cotangent,
    gain_mixer,
    query_weight,
    key_weight,
    value_weight,
    out_weight,
    gain_feed,
    up_weight,
    down_weight,
):
    peer_count = lax.axis_size("patch")
    buffer_rows = 2 * peer_count * SLOTS
    weights = (
        gain_mixer,
        query_weight,
        key_weight,
        value_weight,
        out_weight,
        gain_feed,
        up_weight,
        down_weight,
    )
    pair = jnp.stack([points, cotangent])
    pair = jnp.broadcast_to(pair[None], (lax.axis_size("mp"),) + pair.shape)
    gathered = lax.all_to_all(pair, "mp", split_axis=0, concat_axis=0, tiled=True)
    sent, *kept = first_call(
        patch_counts, gathered, to_hilbert[None, :], weights, buffer_rows
    )
    arrived = exchange_rows(sent)
    hilbert_out, second_keep, second_give, grad_sent = second_call(
        arrived, from_hilbert[None, :], patch_counts[None, :], gathered, weights
    )
    grad_arrived = exchange_rows(grad_sent)
    chips = peer_count // 2
    keep, give = last_call(
        grad_arrived, gathered, kept, (second_keep, second_give), weights, chips,
    )
    taken = swap_cores(give, peer_count)
    terms = (keep.astype(F32) + taken.astype(F32)).astype(BF)
    groups = [[2 * chip + core for chip in range(chips)] for core in range(2)]
    arrived_terms = exchange(terms.reshape(chips, CHUNK_ROWS // 4, 4, LANES), groups)
    sums = jnp.sum(arrived_terms.astype(F32), axis=0).astype(BF).reshape(CHUNK_ROWS, LANES)
    share = CHUNK_ROWS - GAIN_ROWS
    spread = jnp.broadcast_to(sums[None, :share], (chips, share, LANES))
    own = exchange(spread, groups).reshape(chips * share, LANES)
    gain_rows = sums[share:] + own[:GAIN_ROWS] * 0
    own = jnp.concatenate([own, gain_rows, jnp.zeros((16 - GAIN_ROWS, LANES), BF)], axis=0)
    other = swap_cores(own, peer_count)
    return (hilbert_out, *finish_call(own, other))


def solution(mesh):
    split = P(("patch", "mp"), None)
    in_specs = (split, P(), P("patch"), P("patch"), split) + (P(),) * 8
    own_rows = P(None, "mp", None)
    out_specs = (split, P(), own_rows, own_rows, own_rows, own_rows, P(), own_rows, own_rows)
    return jax.shard_map(body, mesh=mesh, in_specs=in_specs, out_specs=out_specs, check_vma=False)
```
